32 devices in a mesh: rows: 16 (over z, x, core), heads: 2 (over y).
Axes of the slice: x: 2, y: 2, z: 4, core: 2. Of those that a mesh axis runs over, the one named last changes fastest.
Arguments:
- hidden: bfloat16 [2, 16, 8192], P(None, None, 'rows'), may hold values from -6 to 6
- norm_gain: bfloat16 [8192], P('rows'), may hold values from 0.5 to 2
- query_weight: bfloat16 [8192, 8192], P('rows', 'heads'), may hold values from -0.0625 to 0.0625
- query_gain: bfloat16 [128], replicated, may hold values from 0.5 to 2
- out_weight: bfloat16 [8192, 8192], P('heads', 'rows'), may hold values from -0.0625 to 0.0625
- attn_gate: float32 [1], replicated, may hold values from 0.3 to 1.5
- kv_cache: bfloat16 [16, 8, 4, 1408, 256], P('rows', 'heads'), may hold values from -384 to 384
- new_tiles: bfloat16 [16, 8, 1408, 256], P('rows', 'heads'), may hold values from -384 to 384
- counts: int32 [2, 16], P(None, 'rows'), may hold values from 1 to 4, as said below
- join_list: int32 [2, 2, 3], replicated, may hold values from 0 to 15, as said below
Outputs:
- mixed: bfloat16 [2, 16, 8192], P(None, None, 'rows')
- arrived: bfloat16 [16, 8, 1408, 256], P('rows', 'heads')
The draws below stay inside these ranges and needn't reach their ends.
Inputs may be any that keep to these rules, and one draw needn't show every extreme that they name: Some row has 4 tiles and some row one tile at each step; a row that receives a tile in slot k at some step counts more than k tiles at that step and every later one. `join_list`: sources are distinct over all entries, below 16; targets are distinct over all entries, below 16; slots are below 4.
All inputs are finite; a program needn't handle non-finite values.
Results may differ from the reference program's by a relative error of at most 0.0045.
The reference program's roundings to bfloat16 on the way count: a program that leaves them out, or rounds other values in their place, can miss the bound.
Values may be sent and summed in bfloat16 or wider, within the bound.
No kernel may reach another device: no remote copies, remote signals or barrier semaphores. Data moves between devices by JAX's collectives and lax.ppermute only.
A program may use at most 128 MiB of HBM per device.

```python
import math
import jax
import jax.numpy as jnp
from jax import lax

D = 8192
HEADS = 64
KV_HEADS = 8
HEAD_DIM = 128
TILE = 1408
SLOTS = 4
STEPS = 2
JOINS = 2
ROWS_DEV = 1
BATCH = 16
ENCODERS = 16


def joint_draw(key):
    keys = jax.random.split(key, 4)
    sources = jax.random.permutation(keys[0], ENCODERS - 2)[:STEPS * JOINS].astype(jnp.int32)
    first_target = (sources[0] + 1) * ROWS_DEV
    spare = jax.random.permutation(keys[1], BATCH - 2).astype(jnp.int32)
    spare = spare + (spare >= first_target).astype(jnp.int32)
    targets = jnp.concatenate([jnp.stack([first_target, jnp.int32(BATCH - 1)]), spare[:STEPS * JOINS - 2]])
    sources = sources.reshape(STEPS, JOINS)
    targets = targets.reshape(STEPS, JOINS)
    slot_draw = jax.random.randint(keys[2], (STEPS, JOINS), 0, SLOTS)
    slot_draw = slot_draw.at[0, 0].set(0)
    base = jax.random.randint(keys[3], (BATCH,), 1, SLOTS + 1)
    base = base.at[spare[BATCH - 3]].set(SLOTS)
    base = base.at[spare[BATCH - 4]].set(1)
    positions = jnp.arange(BATCH, dtype=jnp.int32)
    needed = jnp.zeros((BATCH,), jnp.int32)
    per_step = []
    for section_index in range(STEPS):
        for join_index in range(JOINS):
            hits = positions == targets[section_index, join_index]
            needed = jnp.maximum(needed, jnp.where(hits, slot_draw[section_index, join_index] + 1, 0))
        per_step.append(jnp.maximum(base, needed))
    counts = jnp.stack(per_step).astype(jnp.int32)
    joins = jnp.stack([sources, targets, slot_draw], axis=-1).astype(jnp.int32)
    return (counts, joins)


def key_value_block(key, full_shape, spread_shape, lowest, highest, edge_limit, offset):
    keys = jax.random.split(key, 2)
    base = jax.random.truncated_normal(keys[0], -edge_limit, edge_limit, full_shape, jnp.float32)
    spread = jnp.exp(jax.random.uniform(keys[1], spread_shape, jnp.float32, math.log(lowest), math.log(highest)))
    column = jnp.arange(full_shape[-1]) < full_shape[-1] // 2
    key_part = base * spread
    value_part = 3.0 * base + offset
    return jnp.where(column, key_part, value_part).astype(jnp.bfloat16)


def draw_counts(key, part):
    counts, joins = joint_draw(key)
    return counts


def draw_join_list(key, part):
    counts, joins = joint_draw(key)
    return joins


def draw_kv_cache(key, part):
    key = jax.random.fold_in(key, 11)
    full_shape = (BATCH, KV_HEADS, SLOTS, TILE, 2 * HEAD_DIM)
    spread_shape = (BATCH, KV_HEADS, 1, 1, 1)
    return key_value_block(key, full_shape, spread_shape, 0.25, 2.0, 5.0, -2.0)


def draw_new_tiles(key, part):
    key = jax.random.fold_in(key, 13)
    full_shape = (ENCODERS, KV_HEADS, TILE, 2 * HEAD_DIM)
    spread_shape = (ENCODERS, KV_HEADS, 1, 1)
    return key_value_block(key, full_shape, spread_shape, 0.25, 2.0, 5.0, 2.0)


def block_levels(rng, dims, shards, least, high):
    gain = 1.0
    for dim, parts in shards:
        draws = jax.random.uniform(jax.random.fold_in(jax.random.fold_in(rng, 6), dim), (parts,), jnp.float32, least / len(shards), high / len(shards))
        gain = gain * jnp.repeat(jnp.exp(draws), dims[dim] // parts).reshape((-1,) + (1,) * (len(dims) - 1 - dim))
    return gain


def gaussian(own_key, dims, scale, bound, cuts=(), kind=jnp.bfloat16):
    result = scale * jax.random.normal(own_key, dims, jnp.float32)
    if cuts:
        result = result * block_levels(own_key, dims, cuts, -0.22, 0.18)
    return jnp.clip(result, -bound, bound).astype(kind)


def setup_inputs(seed: int = 0) -> dict:
    key_list = jax.random.split(jax.random.key(seed), 11)
    return {
        "hidden": gaussian(key_list[0], (STEPS, BATCH, D), 1.0, 6.0, ((2, 16),)),
        "norm_gain": jnp.clip(jnp.exp(math.log(2.0) - 1.3862944 * jax.random.uniform(key_list[1], (D,), jnp.float32) ** block_levels(key_list[1], (D,), ((0, 16),), -0.2, 0.2)), 0.5, 2.0).astype(jnp.bfloat16),
        "query_weight": gaussian(key_list[2], (D, HEADS * HEAD_DIM), D ** -0.5, 0.0625, ((0, 16), (1, 2))),
        "query_gain": jnp.clip(jnp.exp(jax.random.uniform(key_list[3], (HEAD_DIM,), jnp.float32, math.log(0.5), math.log(2.0))), 0.5, 2.0).astype(jnp.bfloat16),
        "out_weight": gaussian(key_list[4], (HEADS * HEAD_DIM, D), (HEADS * HEAD_DIM) ** -0.5, 0.0625, ((0, 2), (1, 16))),
        "attn_gate": jnp.clip(jax.random.uniform(key_list[5], (1,), jnp.float32, 0.3, 1.5), 0.3, 1.5),
        "kv_cache": draw_kv_cache(jax.random.fold_in(key_list[10], 71), 0),
        "new_tiles": draw_new_tiles(jax.random.fold_in(key_list[10], 71), 0),
        "counts": draw_counts(jax.random.fold_in(key_list[10], 71), 0),
        "join_list": draw_join_list(jax.random.fold_in(key_list[10], 71), 0),
    }


epsilon = 1e-05

def reference(hidden, norm_gain, query_weight, query_gain, out_weight, attn_gate, kv_cache, new_tiles, counts, join_list):
    kv_state = kv_cache
    arrived = jnp.zeros((BATCH, KV_HEADS, TILE, 2 * HEAD_DIM), jnp.bfloat16)
    group_size = HEADS // KV_HEADS
    anchor = jnp.int32(0)
    outputs = []
    for decode_step in range(STEPS):
        for join_index in range(JOINS):
            source = join_list[decode_step, join_index, 0].astype(jnp.int32)
            target = join_list[decode_step, join_index, 1].astype(jnp.int32)
            slot_index = join_list[decode_step, join_index, 2].astype(jnp.int32)
            new_block = lax.dynamic_index_in_dim(new_tiles, source, 0, keepdims=False)
            kv_state = lax.dynamic_update_slice(kv_state, new_block[None, :, None], (target, anchor, slot_index, anchor, anchor))
            arrived = lax.dynamic_update_slice(arrived, new_block[None], (target, anchor, anchor, anchor))
        tokens = hidden[decode_step].astype(jnp.float32)
        scaled = (tokens * norm_gain.astype(jnp.float32)).astype(jnp.bfloat16)
        queries = jnp.dot(scaled, query_weight, preferred_element_type=jnp.float32)
        queries = queries.reshape(BATCH, HEADS, HEAD_DIM)
        queries = queries * lax.rsqrt(lax.optimization_barrier(jnp.mean(queries * queries, axis=-1, keepdims=True)) + epsilon) * query_gain.astype(jnp.float32)
        queries = queries.astype(jnp.bfloat16).reshape(BATCH, KV_HEADS, group_size, HEAD_DIM)
        lengths = counts[decode_step] * TILE

        def attend(row_index):
            row_cache = lax.dynamic_index_in_dim(kv_state, row_index, 0, keepdims=False)
            row_cache = row_cache.reshape(KV_HEADS, SLOTS * TILE, 2 * HEAD_DIM).astype(jnp.float32)
            row_query = lax.dynamic_index_in_dim(queries, row_index, 0, keepdims=False).astype(jnp.float32)
            scores = jnp.einsum('kgd,ktd->kgt', row_query, row_cache[:, :, :HEAD_DIM]) * (1.0 / math.sqrt(HEAD_DIM))
            limit = lax.dynamic_index_in_dim(lengths, row_index, 0, keepdims=False)
            usable = (jnp.arange(SLOTS * TILE, dtype=jnp.int32) < limit)[None, None, :]
            scores = jnp.where(usable, scores, -1e+30)
            highest = lax.optimization_barrier(jnp.max(scores, axis=-1, keepdims=True))
            exponent = jnp.where(usable, jnp.exp(scores - highest), 0.0)
            probs = (exponent / lax.optimization_barrier(jnp.sum(exponent, axis=-1, keepdims=True))).astype(jnp.bfloat16)
            context = jnp.einsum('kgt,ktd->kgd', probs.astype(jnp.float32), row_cache[:, :, HEAD_DIM:])
            return context.astype(jnp.bfloat16).reshape(HEADS * HEAD_DIM)
        context = lax.map(attend, jnp.arange(BATCH, dtype=jnp.int32))
        projected = jnp.dot(context, out_weight, preferred_element_type=jnp.float32)
        outputs.append((tokens + jnp.tanh(attn_gate[0]) * projected).astype(jnp.bfloat16))
    return (jnp.stack(outputs), arrived)
```

```python
import functools
import math

import jax
import jax.numpy as jnp
from jax import lax
from jax.experimental import pallas as pl
from jax.experimental.pallas import tpu as pltpu
from jax.sharding import PartitionSpec as P

STEPS = 2
JOINS = 2
TOTAL = STEPS * JOINS

epsilon = 1e-05

ROUNDS = [(0, 0, 0, 0), (0, 1, 0, 0), (0, 0, 1, 0), (0, 0, 0, 1),
          (0, 1, 1, 0), (0, 1, 0, 1), (0, 0, 1, 1), (0, 1, 1, 1)]


def plan_kernel(join_ref, plan_ref):
    me = lax.axis_index("rows")
    source, target, slot = [], [], []
    for s in range(STEPS):
        for j in range(JOINS):
            source.append(join_ref[s, j, 0])
            target.append(join_ref[s, j, 1])
            slot.append(join_ref[s, j, 2])
    one, zero = jnp.int32(1), jnp.int32(0)
    clash = {}
    for i in range(TOTAL):
        for j in range(i + 1, TOTAL):
            both = (source[i] == target[j]) | (source[j] == target[i])
            clash[i, j] = jnp.where(both, one, zero)
    best = [jnp.int32(0)] * TOTAL
    found = zero
    for rounds in reversed(ROUNDS):
        bad = zero
        for (i, j), value in clash.items():
            if rounds[i] == rounds[j]:
                bad = bad | value
        good = bad == 0
        found = jnp.where(good, one, found)
        best = [jnp.where(good, jnp.int32(r), b) for r, b in zip(rounds, best)]
    odd = found == 0
    branch = [zero, zero]
    arrives, step, place = zero, jnp.int32(STEPS), zero
    for i in range(TOTAL):
        s, t = source[i], target[i]
        key = s ^ t
        kind = jnp.where(key == 0, 1, 2 + 2 * (key - 1) + jnp.where(s < t, 0, 1))
        part = (me == s) | (me == t)
        for r in range(2):
            branch[r] = jnp.where(part & (best[i] == r), kind, branch[r])
        here = me == t
        arrives = jnp.where(here, best[i] + 1, arrives)
        step = jnp.where(here, i // JOINS, step)
        place = jnp.where(here, slot[i], place)
    plan_ref[0] = jnp.where(odd, zero, branch[0])
    plan_ref[1] = jnp.where(odd, zero, branch[1])
    plan_ref[2] = jnp.where(odd & (arrives > 0), jnp.int32(1), arrives)
    plan_ref[3] = step
    plan_ref[4] = place
    plan_ref[5] = jnp.where(odd, one, zero)


def make_plan(join_list, rows):
    last = 2 + 2 * (rows - 1)
    plan = pl.pallas_call(
        plan_kernel,
        out_shape=jax.ShapeDtypeStruct((8,), jnp.int32),
        in_specs=[pl.BlockSpec(memory_space=pltpu.SMEM)],
        out_specs=pl.BlockSpec(memory_space=pltpu.SMEM),
        name="plan",
    )(join_list)
    return plan, last


def transfer(tile, branch, rows, extra=None):
    def skip(block):
        return jnp.zeros_like(block)

    def keep(block):
        return block

    def send(pairs):
        return lambda block: lax.ppermute(block, "rows", pairs)

    branches = [skip, keep]
    for key in range(1, rows):
        for low in (True, False):
            pairs = [(i, i ^ key) for i in range(rows) if (i < (i ^ key)) == low]
            branches.append(send(pairs))
    if extra is not None:
        branches.append(extra)
    return lax.switch(branch, branches, tile)


def attend_kernel(parts, group, head_size, plan_ref, counts_ref, gain_ref, *refs):
    sums, (kv_ref, new_ref, out_ref) = refs[:parts], refs[parts:]
    slots = kv_ref.shape[2]
    raw = sums[0][...]
    for ref in sums[1:]:
        raw = raw + ref[...]
    raw = jnp.concatenate(
        [raw[:, g * head_size:(g + 1) * head_size] for g in range(group)], axis=0
    )
    queries = (
        raw
        * lax.rsqrt(jnp.mean(raw * raw, axis=-1, keepdims=True) + epsilon)
        * gain_ref[...].astype(jnp.float32)
    ).astype(jnp.bfloat16)
    row = lax.broadcasted_iota(jnp.int32, (group * STEPS, 1), 0)
    second = lax.rem(row, STEPS) == 1
    join_step, join_slot = plan_ref[3], plan_ref[4]
    one, zero = jnp.int32(1), jnp.int32(0)

    def scores_of(keys, shown):
        scores = lax.dot_general(
            queries, keys, (((1,), (1,)), ((), ())), preferred_element_type=jnp.float32
        ) * (1.0 / math.sqrt(head_size))
        usable = jnp.where(second, shown[1], shown[0]) > 0
        return jnp.where(usable, scores, -1e30)

    all_scores = []
    for i in range(slots):
        shown = [
            jnp.where(
                (i < counts_ref[s, 0]) & ((join_step > s) | (join_slot != i)), one, zero
            )
            for s in range(STEPS)
        ]
        all_scores.append(scores_of(kv_ref[0, 0, i, :, :head_size], shown))
    shown = [jnp.where(join_step <= s, one, zero) for s in range(STEPS)]
    all_scores.append(scores_of(new_ref[0, :, :head_size], shown))
    highest = all_scores[0].max(axis=-1, keepdims=True)
    for scores in all_scores[1:]:
        highest = jnp.maximum(highest, scores.max(axis=-1, keepdims=True))
    exponents = [jnp.exp(scores - highest) for scores in all_scores]
    total = exponents[0].sum(axis=-1, keepdims=True)
    for exponent in exponents[1:]:
        total = total + exponent.sum(axis=-1, keepdims=True)
    context = jnp.zeros((group * STEPS, head_size), jnp.float32)
    for i in range(slots + 1):
        probs = (exponents[i] / total).astype(jnp.bfloat16)
        values = new_ref[0, :, head_size:] if i == slots else kv_ref[0, 0, i, :, head_size:]
        context = context + jnp.dot(probs, values, preferred_element_type=jnp.float32)
    context = jnp.concatenate(
        [context[g * STEPS:(g + 1) * STEPS] for g in range(group)], axis=1
    )
    out_ref[...] = context.astype(jnp.bfloat16)


def attend(plan, counts, query_gain, sums, kv_cache, arrived):
    _, kv_here, slots, tile_len, width = kv_cache.shape
    head_size = width // 2
    heads_here = sums[0].shape[1] // head_size
    group = heads_here // kv_here
    wide = group * head_size
    smem = pl.BlockSpec(memory_space=pltpu.SMEM)
    return pl.pallas_call(
        functools.partial(attend_kernel, len(sums), group, head_size),
        grid=(kv_here,),
        out_shape=jax.ShapeDtypeStruct((STEPS, heads_here * head_size), jnp.bfloat16),
        in_specs=[smem, smem, pl.BlockSpec((1, head_size), lambda h: (0, 0))]
        + [pl.BlockSpec((STEPS, wide), lambda h: (0, h)) for _ in sums]
        + [
            pl.BlockSpec((1, 1, slots, tile_len, width), lambda h: (0, h, 0, 0, 0)),
            pl.BlockSpec((1, tile_len, width), lambda h: (h, 0, 0)),
        ],
        out_specs=pl.BlockSpec((STEPS, wide), lambda h: (0, h)),
        compiler_params=pltpu.CompilerParams(vmem_limit_bytes=40 * 1024 * 1024),
        cost_estimate=pl.CostEstimate(
            flops=4 * kv_here * (slots + 1) * tile_len * width * group,
            bytes_accessed=kv_here * (slots + 1) * tile_len * width * 2,
            transcendentals=kv_here * (slots + 1) * tile_len * group * STEPS,
        ),
        name="attend",
    )(plan, counts, query_gain.reshape(1, head_size), *sums, kv_cache, arrived)


def on_device(
    rows,
    heads,
    hidden,
    norm_gain,
    query_weight,
    query_gain,
    out_weight,
    attn_gate,
    kv_cache,
    new_tiles,
    counts,
    join_list,
):
    width = hidden.shape[2]
    me = lax.axis_index("rows")
    chips = rows // 2
    own_tile = new_tiles[0]
    plan, last = make_plan(join_list, rows)

    order = jnp.arange(rows, dtype=jnp.int32) ^ me
    shuffle = (order[:, None] == jnp.arange(rows, dtype=jnp.int32)[None, :])
    shuffle = shuffle.astype(jnp.bfloat16)
    wide_hidden = hidden.astype(jnp.float32)
    scaled = (wide_hidden * norm_gain.astype(jnp.float32)).astype(jnp.bfloat16)
    scaled = jnp.einsum(
        "kb,sbd->ksd", shuffle, scaled, preferred_element_type=jnp.float32
    ).astype(jnp.bfloat16)
    partial = jnp.dot(
        scaled.reshape(rows * STEPS, width), query_weight, preferred_element_type=jnp.float32
    )
    columns = partial.shape[1]
    partial = partial.reshape(chips, 2, STEPS, columns)

    def across(block, axis, size, key):
        return lax.ppermute(block, axis, [(i, i ^ key) for i in range(size)])

    pair = partial[:, 0] + across(partial[:, 1], "rows", rows, 1)
    sums = [pair[0]] + [across(pair[k], "rows", rows, 2 * k) for k in range(1, chips)]

    def summed(block):
        result = jnp.zeros_like(block)
        for s in range(STEPS):
            for j in range(JOINS):
                given = jnp.where(me == join_list[s, j, 0], block, jnp.zeros_like(block))
                given = lax.psum(given, "rows")
                result = jnp.where(me == join_list[s, j, 1], given, result)
        return result

    first = transfer(
        own_tile, jnp.where(plan[5] > 0, last, plan[0]), rows, summed
    )
    other = transfer(own_tile, plan[1], rows)
    arrived = jnp.where(
        plan[2] == 1, first, jnp.where(plan[2] == 2, other, jnp.zeros_like(own_tile))
    )
    context = attend(plan, counts, query_gain, sums, kv_cache, arrived)
    gathered = jnp.stack(
        [context] + [across(context, "rows", rows, 2 * k) for k in range(1, chips)]
    )
    gathered = jnp.stack([gathered, across(gathered, "rows", rows, 1)], axis=1)
    gathered = gathered.reshape(rows * STEPS, columns)
    projected = jnp.dot(gathered, out_weight, preferred_element_type=jnp.float32)
    key = 1
    while key < heads:
        projected = projected + across(projected, "heads", heads, key)
        key *= 2
    projected = projected.reshape(rows, STEPS, width)
    bit = 1
    while bit < rows:
        split = projected.reshape(rows // (2 * bit), 2, bit, STEPS, width)
        projected = jnp.where((me & bit) > 0, split[:, ::-1], split)
        bit *= 2
    projected = projected.reshape(rows, STEPS, width).transpose(1, 0, 2)
    mixed = (wide_hidden + jnp.tanh(attn_gate[0]) * projected).astype(jnp.bfloat16)
    return mixed, arrived[None]


def solution(mesh):
    in_specs = (
        P(None, None, "rows"),
        P("rows"),
        P("rows", "heads"),
        P(),
        P("heads", "rows"),
        P(),
        P("rows", "heads", None, None, None),
        P("rows", "heads", None, None),
        P(None, "rows"),
        P(),
    )
    out_specs = (P(None, None, "rows"), P("rows", "heads", None, None))
    body = functools.partial(on_device, mesh.shape["rows"], mesh.shape["heads"])
    return jax.shard_map(
        body, mesh=mesh, in_specs=in_specs, out_specs=out_specs, check_vma=False
    )
```

```python
import functools
import math

import jax
import jax.numpy as jnp
from jax import lax
from jax.experimental import pallas as pl
from jax.experimental.pallas import tpu as pltpu
from jax.sharding import PartitionSpec as P

STEPS = 2
JOINS = 2
TOTAL = STEPS * JOINS

epsilon = 1e-05

ROUNDS = [(0, 0, 0, 0), (0, 1, 0, 0), (0, 0, 1, 0), (0, 0, 0, 1),
          (0, 1, 1, 0), (0, 1, 0, 1), (0, 0, 1, 1), (0, 1, 1, 1)]


def plan_kernel(join_ref, plan_ref):
    me = lax.axis_index("rows")
    rows = lax.axis_size("rows")
    source, target, slot = [], [], []
    for s in range(STEPS):
        for j in range(JOINS):
            source.append(join_ref[s, j, 0])
            target.append(join_ref[s, j, 1])
            slot.append(join_ref[s, j, 2])
    one, zero = jnp.int32(1), jnp.int32(0)

    busy = []
    for i in range(TOTAL):
        for sender in (source[i], source[i] ^ 1):
            hit = zero
            for j in range(TOTAL):
                if j != i:
                    hit = hit | jnp.where(sender == target[j], one, zero)
            busy.append(hit)
    same = {}
    for i in range(TOTAL):
        for j in range(i + 1, TOTAL):
            same[i, j] = jnp.where(source[i] == (source[j] ^ 1), one, zero)
    single = zero
    swap = [zero] * TOTAL
    choices = sorted(range(2 ** TOTAL), key=lambda m: (-bin(m).count("1"), m))
    for m in choices:
        bits = [(m >> i) & 1 for i in range(TOTAL)]
        bad = zero
        for i in range(TOTAL):
            bad = bad | busy[2 * i + bits[i]]
        for (i, j), value in same.items():
            if bits[i] != bits[j]:
                bad = bad | value
        good = bad == 0
        single = jnp.where(good, one, single)
        swap = [jnp.where(good, jnp.int32(b), w) for b, w in zip(bits, swap)]

    clash = {}
    for i in range(TOTAL):
        for j in range(i + 1, TOTAL):
            both = (source[i] == target[j]) | (source[j] == target[i])
            clash[i, j] = jnp.where(both, one, zero)
    best = [zero] * TOTAL
    double = zero
    for rounds in reversed(ROUNDS):
        bad = zero
        for (i, j), value in clash.items():
            if rounds[i] == rounds[j]:
                bad = bad | value
        good = bad == 0
        double = jnp.where(good, one, double)
        best = [jnp.where(good, jnp.int32(r), b) for r, b in zip(rounds, best)]

    def kind_of(s, t):
        key = s ^ t
        return jnp.where(key == 0, 1, 2 * key + jnp.where(s < t, 0, 1))

    only, branch = zero, [zero, zero]
    arrives, step, place = zero, jnp.int32(STEPS), zero
    for i in range(TOTAL):
        s, t = source[i], target[i]
        sender = s ^ swap[i]
        part = (me == sender) | (me == t)
        only = jnp.where(part, kind_of(sender, t) + swap[i] * (2 * rows - 1), only)
        part = (me == s) | (me == t)
        for r in range(2):
            branch[r] = jnp.where(part & (best[i] == r), kind_of(s, t), branch[r])
        here = me == t
        arrives = jnp.where(here, best[i] + 1, arrives)
        step = jnp.where(here, i // JOINS, step)
        place = jnp.where(here, slot[i], place)
    plan_ref[0] = only
    plan_ref[1] = branch[0]
    plan_ref[2] = branch[1]
    plan_ref[3] = step
    plan_ref[4] = place
    plan_ref[5] = jnp.where(single > 0, 0, jnp.where(double > 0, 1, 2))
    plan_ref[6] = arrives
    plan_ref[7] = zero


def make_plan(join_list):
    return pl.pallas_call(
        plan_kernel,
        out_shape=jax.ShapeDtypeStruct((8,), jnp.int32),
        in_specs=[pl.BlockSpec(memory_space=pltpu.SMEM)],
        out_specs=pl.BlockSpec(memory_space=pltpu.SMEM),
        name="plan",
    )(join_list)


def transfer(branch, rows, *tiles):
    branches = [lambda *blocks: jnp.zeros_like(blocks[0])]

    def keep(index):
        return lambda *blocks: blocks[index]

    def send(index, pairs):
        return lambda *blocks: lax.ppermute(blocks[index], "rows", pairs)

    for index in range(len(tiles)):
        branches.append(keep(index))
        for key in range(1, rows):
            for low in (True, False):
                pairs = [(i, i ^ key) for i in range(rows) if (i < (i ^ key)) == low]
                branches.append(send(index, pairs))
    return lax.switch(branch, branches, *tiles)


def move_tiles(plan, join_list, rows, own, other):
    me = lax.axis_index("rows")

    def once(own, other):
        return transfer(plan[0], rows, own, other)

    def twice(own, other):
        first = transfer(plan[1], rows, own)
        second = transfer(plan[2], rows, own)
        late = plan[6] == 2
        return jnp.where(plan[6] == 1, first, jnp.where(late, second, jnp.zeros_like(own)))

    def summed(own, other):
        result = jnp.zeros_like(own)
        for s in range(STEPS):
            for j in range(JOINS):
                given = jnp.where(me == join_list[s, j, 0], own, jnp.zeros_like(own))
                given = lax.psum(given, "rows")
                result = jnp.where(me == join_list[s, j, 1], given, result)
        return result

    return lax.switch(plan[5], [once, twice, summed], own, other)


def attend_kernel(group, head_size, plan_ref, counts_ref, gain_ref, sums_ref, kv_ref, new_ref, out_ref, kept_ref):
    kept_ref[...] = new_ref[...]
    slots = kv_ref.shape[2]
    raw = sums_ref[0]
    for k in range(1, sums_ref.shape[0]):
        raw = raw + sums_ref[k]
    raw = jnp.concatenate(
        [raw[:, g * head_size:(g + 1) * head_size] for g in range(group)], axis=0
    )
    queries = (
        raw
        * lax.rsqrt(jnp.mean(raw * raw, axis=-1, keepdims=True) + epsilon)
        * gain_ref[...].astype(jnp.float32)
    ).astype(jnp.bfloat16)
    row = lax.broadcasted_iota(jnp.int32, (group * STEPS, 1), 0)
    second = lax.rem(row, STEPS) == 1
    join_step, join_slot = plan_ref[3], plan_ref[4]
    one, zero = jnp.int32(1), jnp.int32(0)

    def scores_of(keys, shown):
        scores = lax.dot_general(
            queries, keys, (((1,), (1,)), ((), ())), preferred_element_type=jnp.float32
        ) * (1.0 / math.sqrt(head_size))
        usable = jnp.where(second, shown[1], shown[0]) > 0
        return jnp.where(usable, scores, -1e30)

    all_scores = []
    for i in range(slots):
        shown = [
            jnp.where(
                (i < counts_ref[s, 0]) & ((join_step > s) | (join_slot != i)), one, zero
            )
            for s in range(STEPS)
        ]
        all_scores.append(scores_of(kv_ref[0, 0, i, :, :head_size], shown))
    shown = [jnp.where(join_step <= s, one, zero) for s in range(STEPS)]
    all_scores.append(scores_of(new_ref[0, :, :head_size], shown))
    highest = all_scores[0].max(axis=-1, keepdims=True)
    for scores in all_scores[1:]:
        highest = jnp.maximum(highest, scores.max(axis=-1, keepdims=True))
    exponents = [jnp.exp(scores - highest) for scores in all_scores]
    total = exponents[0].sum(axis=-1, keepdims=True)
    for exponent in exponents[1:]:
        total = total + exponent.sum(axis=-1, keepdims=True)
    context = jnp.zeros((group * STEPS, head_size), jnp.float32)
    for i in range(slots + 1):
        probs = (exponents[i] / total).astype(jnp.bfloat16)
        values = new_ref[0, :, head_size:] if i == slots else kv_ref[0, 0, i, :, head_size:]
        context = context + jnp.dot(probs, values, preferred_element_type=jnp.float32)
    context = jnp.concatenate(
        [context[g * STEPS:(g + 1) * STEPS] for g in range(group)], axis=1
    )
    out_ref[...] = context.astype(jnp.bfloat16)


def attend(plan, counts, query_gain, sums, kv_cache, arrived):
    _, kv_here, slots, tile_len, width = kv_cache.shape
    head_size = width // 2
    chips, _, columns = sums.shape
    heads_here = columns // head_size
    group = heads_here // kv_here
    wide = group * head_size
    smem = pl.BlockSpec(memory_space=pltpu.SMEM)
    return pl.pallas_call(
        functools.partial(attend_kernel, group, head_size),
        grid=(kv_here,),
        out_shape=(
            jax.ShapeDtypeStruct((STEPS, heads_here * head_size), jnp.bfloat16),
            jax.ShapeDtypeStruct(arrived.shape, jnp.bfloat16),
        ),
        in_specs=[
            smem,
            smem,
            pl.BlockSpec((1, head_size), lambda h: (0, 0)),
            pl.BlockSpec((chips, STEPS, wide), lambda h: (0, 0, h)),
            pl.BlockSpec((1, 1, slots, tile_len, width), lambda h: (0, h, 0, 0, 0)),
            pl.BlockSpec((1, tile_len, width), lambda h: (h, 0, 0)),
        ],
        out_specs=(
            pl.BlockSpec((STEPS, wide), lambda h: (0, h)),
            pl.BlockSpec((1, tile_len, width), lambda h: (h, 0, 0)),
        ),
        compiler_params=pltpu.CompilerParams(vmem_limit_bytes=53 * 1024 * 1024),
        cost_estimate=pl.CostEstimate(
            flops=4 * kv_here * (slots + 1) * tile_len * width * group,
            bytes_accessed=kv_here * (slots + 1) * tile_len * width * 2,
            transcendentals=kv_here * (slots + 1) * tile_len * group * STEPS,
        ),
        name="attend",
    )(plan, counts, query_gain.reshape(1, head_size), sums, kv_cache, arrived)


def on_device(
    rows,
    heads,
    hidden,
    norm_gain,
    query_weight,
    query_gain,
    out_weight,
    attn_gate,
    kv_cache,
    new_tiles,
    counts,
    join_list,
):
    width = hidden.shape[2]
    me = lax.axis_index("rows")
    odd = (me & 1) > 0
    chips = rows // 2
    own_tile = new_tiles[0]
    plan = make_plan(join_list)

    def across(block, axis, size, key):
        return lax.ppermute(block, axis, [(i, i ^ key) for i in range(size)])

    same_core = [list(range(core, rows, 2)) for core in range(2)]

    def between_chips(blocks):
        return lax.all_to_all(blocks, "rows", 0, 0, axis_index_groups=same_core, tiled=True)

    other_tile = across(own_tile, "rows", rows, 1)
    wide_hidden = hidden.astype(jnp.float32)
    scaled = (wide_hidden * norm_gain.astype(jnp.float32)).astype(jnp.bfloat16)
    scaled = scaled.reshape(STEPS, chips, 2, width).transpose(2, 1, 0, 3)
    scaled = jnp.where(odd, scaled[::-1], scaled)
    partial = jnp.dot(
        scaled.reshape(rows * STEPS, width), query_weight, preferred_element_type=jnp.float32
    )
    columns = partial.shape[1]
    partial = partial.reshape(2, chips, STEPS, columns)
    sums = between_chips(partial[0] + across(partial[1], "rows", rows, 1))
    arrived = move_tiles(plan, join_list, rows, own_tile, other_tile)
    context, arrived = attend(plan, counts, query_gain, sums, kv_cache, arrived)
    mine = between_chips(jnp.broadcast_to(context, (chips, STEPS, columns)))
    theirs = across(mine, "rows", rows, 1)
    gathered = jnp.stack(
        [jnp.where(odd, theirs, mine), jnp.where(odd, mine, theirs)], axis=1
    )
    gathered = gathered.transpose(2, 0, 1, 3).reshape(STEPS * rows, columns)
    projected = jnp.dot(gathered, out_weight, preferred_element_type=jnp.float32)
    key = 1
    while key < heads:
        projected = projected + across(projected, "heads", heads, key)
        key *= 2
    projected = projected.reshape(STEPS, rows, width)
    mixed = (wide_hidden + jnp.tanh(attn_gate[0]) * projected).astype(jnp.bfloat16)
    return mixed, arrived[None]


def solution(mesh):
    in_specs = (
        P(None, None, "rows"),
        P("rows"),
        P("rows", "heads"),
        P(),
        P("heads", "rows"),
        P(),
        P("rows", "heads", None, None, None),
        P("rows", "heads", None, None),
        P(None, "rows"),
        P(),
    )
    out_specs = (P(None, None, "rows"), P("rows", "heads", None, None))
    body = functools.partial(on_device, mesh.shape["rows"], mesh.shape["heads"])
    return jax.shard_map(
        body, mesh=mesh, in_specs=in_specs, out_specs=out_specs, check_vma=False
    )
```

```python
import functools
import math

import jax
import jax.numpy as jnp
from jax import lax
from jax.experimental import pallas as pl
from jax.experimental.pallas import tpu as pltpu
from jax.sharding import PartitionSpec as P

STEPS = 2
JOINS = 2
TOTAL = STEPS * JOINS

epsilon = 1e-05

ROUNDS = [(0, 0, 0, 0), (0, 1, 0, 0), (0, 0, 1, 0), (0, 0, 0, 1),
          (0, 1, 1, 0), (0, 1, 0, 1), (0, 0, 1, 1), (0, 1, 1, 1)]


def write_plan(rows, join_ref, only_ref, way_ref, plan_ref):
    me = lax.axis_index("rows")
    source, target, slot = [], [], []
    for s in range(STEPS):
        for j in range(JOINS):
            source.append(join_ref[s, j, 0])
            target.append(join_ref[s, j, 1])
            slot.append(join_ref[s, j, 2])
    one, zero = jnp.int32(1), jnp.int32(0)

    busy = []
    for i in range(TOTAL):
        for sender in (source[i], source[i] ^ 1):
            hit = zero
            for j in range(TOTAL):
                if j != i:
                    hit = hit | jnp.where(sender == target[j], one, zero)
            busy.append(hit)
    same = {}
    for i in range(TOTAL):
        for j in range(i + 1, TOTAL):
            same[i, j] = jnp.where(source[i] == (source[j] ^ 1), one, zero)
    single = zero
    swap = [zero] * TOTAL
    choices = sorted(range(2 ** TOTAL), key=lambda m: (-bin(m).count("1"), m))
    for m in choices:
        bits = [(m >> i) & 1 for i in range(TOTAL)]
        bad = zero
        for i in range(TOTAL):
            bad = bad | busy[2 * i + bits[i]]
        for (i, j), value in same.items():
            if bits[i] != bits[j]:
                bad = bad | value
        good = bad == 0
        single = jnp.where(good, one, single)
        swap = [jnp.where(good, jnp.int32(b), w) for b, w in zip(bits, swap)]

    clash = {}
    for i in range(TOTAL):
        for j in range(i + 1, TOTAL):
            both = (source[i] == target[j]) | (source[j] == target[i])
            clash[i, j] = jnp.where(both, one, zero)
    best = [zero] * TOTAL
    double = zero
    for rounds in reversed(ROUNDS):
        bad = zero
        for (i, j), value in clash.items():
            if rounds[i] == rounds[j]:
                bad = bad | value
        good = bad == 0
        double = jnp.where(good, one, double)
        best = [jnp.where(good, jnp.int32(r), b) for r, b in zip(rounds, best)]

    def kind_of(s, t):
        key = s ^ t
        return jnp.where(key == 0, 1, 2 * key + jnp.where(s < t, 0, 1))

    only, branch = zero, [zero, zero]
    arrives, step, place = zero, jnp.int32(STEPS), zero
    for i in range(TOTAL):
        s, t = source[i], target[i]
        sender = s ^ swap[i]
        part = (me == sender) | (me == t)
        only = jnp.where(part, kind_of(sender, t) + swap[i] * (2 * rows - 1), only)
        part = (me == s) | (me == t)
        for r in range(2):
            branch[r] = jnp.where(part & (best[i] == r), kind_of(s, t), branch[r])
        here = me == t
        arrives = jnp.where(here, best[i] + 1, arrives)
        step = jnp.where(here, i // JOINS, step)
        place = jnp.where(here, slot[i], place)
    only_ref[0] = only
    way_ref[0] = jnp.where(single > 0, 0, jnp.where(double > 0, 1, 2))
    plan_ref[0] = branch[0]
    plan_ref[1] = branch[1]
    plan_ref[2] = arrives
    plan_ref[3] = step
    plan_ref[4] = place
    for i in range(5, 8):
        plan_ref[i] = zero


def project_kernel(
    rows, head_size, join_ref, hidden_ref, gain_ref, weight_ref,
    keep_ref, send_ref, only_ref, way_ref, plan_ref, scaled_ref,
):
    chips = rows // 2

    @pl.when(pl.program_id(0) == 0)
    def _():
        write_plan(rows, join_ref, only_ref, way_ref, plan_ref)
        scaled = hidden_ref[...].astype(jnp.float32) * gain_ref[...].astype(jnp.float32)
        scaled = scaled.astype(jnp.bfloat16)
        count = STEPS * rows
        to = lax.broadcasted_iota(jnp.int32, (count, count), 0)
        given = lax.broadcasted_iota(jnp.int32, (count, count), 1)
        core = (to // (STEPS * chips)) ^ (lax.axis_index("rows") & 1)
        wanted = lax.rem(to // chips, STEPS) * rows + lax.rem(to, chips) * 2 + core
        shuffle = jnp.where(given == wanted, 1.0, 0.0).astype(jnp.bfloat16)
        scaled_ref[...] = jnp.dot(
            shuffle, scaled, preferred_element_type=jnp.float32
        ).astype(jnp.bfloat16)

    product = jnp.dot(scaled_ref[...], weight_ref[...], preferred_element_type=jnp.float32)
    for h in range(weight_ref.shape[1] // head_size):
        piece = product[:, h * head_size:(h + 1) * head_size]
        for s in range(STEPS):
            keep_ref[:, s, h, :] = piece[s * chips:(s + 1) * chips]
            start = (STEPS + s) * chips
            send_ref[:, s, h, :] = piece[start:start + chips]


def project(rows, head_size, join_list, hidden, norm_gain, query_weight):
    width, columns = query_weight.shape
    chips = rows // 2
    heads_here = columns // head_size
    parts = 4 if heads_here % 32 == 0 else 1
    smem = pl.BlockSpec(memory_space=pltpu.SMEM)
    block = pl.BlockSpec((chips, STEPS, heads_here // parts, head_size), lambda i: (0, 0, i, 0))
    sums = jax.ShapeDtypeStruct((chips, STEPS, heads_here, head_size), jnp.float32)
    return pl.pallas_call(
        functools.partial(project_kernel, rows, head_size),
        grid=(parts,),
        out_shape=(
            sums,
            sums,
            jax.ShapeDtypeStruct((1,), jnp.int32),
            jax.ShapeDtypeStruct((1,), jnp.int32),
            jax.ShapeDtypeStruct((8,), jnp.int32),
        ),
        in_specs=[
            smem,
            pl.BlockSpec((STEPS * rows, width), lambda i: (0, 0)),
            pl.BlockSpec((1, width), lambda i: (0, 0)),
            pl.BlockSpec((width, columns // parts), lambda i: (0, i)),
        ],
        out_specs=(block, block, smem, smem, smem),
        scratch_shapes=[pltpu.VMEM((STEPS * rows, width), jnp.bfloat16)],
        compiler_params=pltpu.CompilerParams(vmem_limit_bytes=60 * 1024 * 1024),
        cost_estimate=pl.CostEstimate(
            flops=2 * STEPS * rows * width * columns,
            bytes_accessed=2 * width * columns + 4 * STEPS * rows * columns,
            transcendentals=0,
        ),
        name="project",
    )(join_list, hidden.reshape(STEPS * rows, width), norm_gain.reshape(1, width), query_weight)


def transfer(branch, rows, *tiles):
    branches = [lambda *blocks: jnp.zeros_like(blocks[0])]

    def keep(index):
        return lambda *blocks: blocks[index]

    def send(index, pairs):
        return lambda *blocks: lax.ppermute(blocks[index], "rows", pairs)

    for index in range(len(tiles)):
        branches.append(keep(index))
        for key in range(1, rows):
            for low in (True, False):
                pairs = [(i, i ^ key) for i in range(rows) if (i < (i ^ key)) == low]
                branches.append(send(index, pairs))
    return lax.switch(branch, branches, *tiles)


def move_tiles(only, way, plan, join_list, rows, own, other):
    me = lax.axis_index("rows")

    def once(own, other):
        return transfer(only[0], rows, own, other)

    def twice(own, other):
        first = transfer(plan[0], rows, own)
        second = transfer(plan[1], rows, own)
        late = plan[2] == 2
        return jnp.where(plan[2] == 1, first, jnp.where(late, second, jnp.zeros_like(own)))

    def summed(own, other):
        result = jnp.zeros_like(own)
        for s in range(STEPS):
            for j in range(JOINS):
                given = jnp.where(me == join_list[s, j, 0], own, jnp.zeros_like(own))
                given = lax.psum(given, "rows")
                result = jnp.where(me == join_list[s, j, 1], given, result)
        return result

    return lax.switch(way[0], [once, twice, summed], own, other)


def attend_kernel(slots, group, head_size, plan_ref, counts_ref, gain_ref, sums_ref, *refs):
    kv_refs, (new_ref, out_ref, kept_ref) = refs[:slots], refs[slots:]
    join_step, join_slot = plan_ref[3], plan_ref[4]
    one, zero = jnp.int32(1), jnp.int32(0)
    raw = sums_ref[0]
    for k in range(1, sums_ref.shape[0]):
        raw = raw + sums_ref[k]
    raw = raw.reshape(STEPS * group, head_size)
    queries = (
        raw
        * lax.rsqrt(jnp.mean(raw * raw, axis=-1, keepdims=True) + epsilon)
        * gain_ref[...].astype(jnp.float32)
    ).astype(jnp.bfloat16)
    step = lax.broadcasted_iota(jnp.int32, (STEPS * group, 1), 0) // group

    def scores_of(keys, shown):
        scores = lax.dot_general(
            queries, keys, (((1,), (1,)), ((), ())), preferred_element_type=jnp.float32
        ) * (1.0 / math.sqrt(head_size))
        usable = jnp.where(step == 1, shown[1], shown[0]) > 0
        return jnp.where(usable, scores, -1e30)

    tiles = [ref.at[0, 0, 0] for ref in kv_refs] + [new_ref.at[0]]
    all_scores = []
    for i in range(slots):
        shown = [
            jnp.where(
                (i < counts_ref[s, 0]) & ((join_step > s) | (join_slot != i)), one, zero
            )
            for s in range(STEPS)
        ]
        all_scores.append(scores_of(tiles[i][:, :head_size], shown))
    shown = [jnp.where(join_step <= s, one, zero) for s in range(STEPS)]
    all_scores.append(scores_of(tiles[slots][:, :head_size], shown))
    highest = all_scores[0].max(axis=-1, keepdims=True)
    for scores in all_scores[1:]:
        highest = jnp.maximum(highest, scores.max(axis=-1, keepdims=True))
    exponents = [jnp.exp(scores - highest) for scores in all_scores]
    total = exponents[0].sum(axis=-1, keepdims=True)
    for exponent in exponents[1:]:
        total = total + exponent.sum(axis=-1, keepdims=True)
    context = jnp.zeros((STEPS * group, head_size), jnp.float32)
    for tile, exponent in zip(tiles, exponents):
        probs = (exponent / total).astype(jnp.bfloat16)
        context = context + jnp.dot(
            probs, tile[:, head_size:], preferred_element_type=jnp.float32
        )
    for g in range(group):
        for s in range(STEPS):
            r = s * group + g
            out_ref[s:s + 1, g * head_size:(g + 1) * head_size] = context[r:r + 1]

    @pl.when(join_step < STEPS)
    def _():
        kept_ref[...] = new_ref[...]

    @pl.when(join_step >= STEPS)
    def _():
        kept_ref[...] = jnp.zeros_like(kept_ref)


def attend(plan, counts, query_gain, sums, kv_cache, arrived):
    _, kv_here, slots, tile_len, width = kv_cache.shape
    chips, _, heads_here, head_size = sums.shape
    group = heads_here // kv_here

    def slot_map(i):
        def index_map(h, plan_ref, counts_ref):
            shown = (i < counts_ref[0, 0]) & ((plan_ref[3] > 0) | (plan_ref[4] != i))
            shown = shown | ((i < counts_ref[1, 0]) & ((plan_ref[3] > 1) | (plan_ref[4] != i)))
            return (0, jnp.where(shown, h, 0), i, 0, 0)

        return pl.BlockSpec((1, 1, 1, tile_len, width), index_map)

    def new_map(h, plan_ref, counts_ref):
        return (jnp.where(plan_ref[3] < STEPS, h, 0), 0, 0)

    return pl.pallas_call(
        functools.partial(attend_kernel, slots, group, head_size),
        grid_spec=pltpu.PrefetchScalarGridSpec(
            num_scalar_prefetch=2,
            grid=(kv_here,),
            in_specs=[
                pl.BlockSpec((1, head_size), lambda h, *_: (0, 0)),
                pl.BlockSpec((chips, STEPS, group, head_size), lambda h, *_: (0, 0, h, 0)),
            ]
            + [slot_map(i) for i in range(slots)]
            + [pl.BlockSpec((1, tile_len, width), new_map)],
            out_specs=(
                pl.BlockSpec((STEPS, group * head_size), lambda h, *_: (0, h)),
                pl.BlockSpec((1, tile_len, width), lambda h, *_: (h, 0, 0)),
            ),
        ),
        out_shape=(
            jax.ShapeDtypeStruct((STEPS, heads_here * head_size), jnp.float32),
            jax.ShapeDtypeStruct(arrived.shape, jnp.bfloat16),
        ),
        compiler_params=pltpu.CompilerParams(vmem_limit_bytes=53 * 1024 * 1024),
        cost_estimate=pl.CostEstimate(
            flops=4 * kv_here * (slots + 1) * tile_len * width * group,
            bytes_accessed=kv_here * (slots + 1) * tile_len * width * 2,
            transcendentals=kv_here * (slots + 1) * tile_len * group * STEPS,
        ),
        name="attend",
    )(plan, counts, query_gain.reshape(1, head_size), sums, *([kv_cache] * slots), arrived)


def on_device(
    rows,
    heads,
    hidden,
    norm_gain,
    query_weight,
    query_gain,
    out_weight,
    attn_gate,
    kv_cache,
    new_tiles,
    counts,
    join_list,
):
    width = hidden.shape[2]
    me = lax.axis_index("rows")
    odd = (me & 1) > 0
    chips = rows // 2
    own_tile = new_tiles[0]

    def across(block, axis, size, key):
        return lax.ppermute(block, axis, [(i, i ^ key) for i in range(size)])

    same_core = [list(range(core, rows, 2)) for core in range(2)]

    def between_chips(blocks):
        return lax.all_to_all(blocks, "rows", 0, 0, axis_index_groups=same_core, tiled=True)

    other_tile = across(own_tile, "rows", rows, 1)
    head_size = kv_cache.shape[4] // 2
    columns = query_weight.shape[1]
    keep, send, only, way, plan = project(
        rows, head_size, join_list, hidden, norm_gain, query_weight
    )
    sums = between_chips(keep + across(send, "rows", rows, 1))
    arrived = move_tiles(only, way, plan, join_list, rows, own_tile, other_tile)
    context, arrived = attend(plan, counts, query_gain, sums, kv_cache, arrived)
    context = context.astype(jnp.bfloat16)
    mine = between_chips(jnp.broadcast_to(context, (chips, STEPS, columns)))
    theirs = across(mine, "rows", rows, 1)
    gathered = jnp.stack(
        [jnp.where(odd, theirs, mine), jnp.where(odd, mine, theirs)], axis=1
    )
    gathered = gathered.transpose(2, 0, 1, 3).reshape(STEPS * rows, columns)
    projected = jnp.dot(gathered, out_weight, preferred_element_type=jnp.float32)
    key = 1
    while key < heads:
        projected = projected + across(projected, "heads", heads, key)
        key *= 2
    projected = projected.reshape(STEPS, rows, width)
    mixed = (hidden.astype(jnp.float32) + jnp.tanh(attn_gate[0]) * projected).astype(jnp.bfloat16)
    return mixed, arrived[None]


def solution(mesh):
    in_specs = (
        P(None, None, "rows"),
        P("rows"),
        P("rows", "heads"),
        P(),
        P("heads", "rows"),
        P(),
        P("rows", "heads", None, None, None),
        P("rows", "heads", None, None),
        P(None, "rows"),
        P(),
    )
    out_specs = (P(None, None, "rows"), P("rows", "heads", None, None))
    body = functools.partial(on_device, mesh.shape["rows"], mesh.shape["heads"])
    return jax.shard_map(
        body, mesh=mesh, in_specs=in_specs, out_specs=out_specs, check_vma=False
    )
```

```python
import functools
import math

import jax
import jax.numpy as jnp
from jax import lax
from jax.experimental import pallas as pl
from jax.experimental.pallas import tpu as pltpu
from jax.sharding import PartitionSpec as P

STEPS = 2
JOINS = 2
TOTAL = STEPS * JOINS

epsilon = 1e-05

ROUNDS = [(0, 0, 0, 0), (0, 1, 0, 0), (0, 0, 1, 0), (0, 0, 0, 1),
          (0, 1, 1, 0), (0, 1, 0, 1), (0, 0, 1, 1), (0, 1, 1, 1)]


def write_plan(rows, join_ref, only_ref, way_ref, plan_ref):
    me = lax.axis_index("rows")
    source, target, slot = [], [], []
    for s in range(STEPS):
        for j in range(JOINS):
            source.append(join_ref[s, j, 0])
            target.append(join_ref[s, j, 1])
            slot.append(join_ref[s, j, 2])
    one, zero = jnp.int32(1), jnp.int32(0)

    busy = []
    for i in range(TOTAL):
        for sender in (source[i], source[i] ^ 1):
            hit = zero
            for j in range(TOTAL):
                if j != i:
                    hit = hit | jnp.where(sender == target[j], one, zero)
            busy.append(hit)
    same = {}
    for i in range(TOTAL):
        for j in range(i + 1, TOTAL):
            same[i, j] = jnp.where(source[i] == (source[j] ^ 1), one, zero)
    single = zero
    swap = [zero] * TOTAL
    choices = sorted(range(2 ** TOTAL), key=lambda m: (-bin(m).count("1"), m))
    for m in choices:
        bits = [(m >> i) & 1 for i in range(TOTAL)]
        bad = zero
        for i in range(TOTAL):
            bad = bad | busy[2 * i + bits[i]]
        for (i, j), value in same.items():
            if bits[i] != bits[j]:
                bad = bad | value
        good = bad == 0
        single = jnp.where(good, one, single)
        swap = [jnp.where(good, jnp.int32(b), w) for b, w in zip(bits, swap)]

    clash = {}
    for i in range(TOTAL):
        for j in range(i + 1, TOTAL):
            both = (source[i] == target[j]) | (source[j] == target[i])
            clash[i, j] = jnp.where(both, one, zero)
    best = [zero] * TOTAL
    double = zero
    for rounds in reversed(ROUNDS):
        bad = zero
        for (i, j), value in clash.items():
            if rounds[i] == rounds[j]:
                bad = bad | value
        good = bad == 0
        double = jnp.where(good, one, double)
        best = [jnp.where(good, jnp.int32(r), b) for r, b in zip(rounds, best)]

    def kind_of(s, t):
        key = s ^ t
        return jnp.where(key == 0, 1, 2 * key + jnp.where(s < t, 0, 1))

    only, branch = zero, [zero, zero]
    arrives, step, place = zero, jnp.int32(STEPS), zero
    for i in range(TOTAL):
        s, t = source[i], target[i]
        sender = s ^ swap[i]
        part = (me == sender) | (me == t)
        only = jnp.where(part, kind_of(sender, t) + swap[i] * (2 * rows - 1), only)
        part = (me == s) | (me == t)
        for r in range(2):
            branch[r] = jnp.where(part & (best[i] == r), kind_of(s, t), branch[r])
        here = me == t
        arrives = jnp.where(here, best[i] + 1, arrives)
        step = jnp.where(here, i // JOINS, step)
        place = jnp.where(here, slot[i], place)
    only_ref[0] = only
    way_ref[0] = jnp.where(single > 0, 0, jnp.where(double > 0, 1, 2))
    plan_ref[0] = branch[0]
    plan_ref[1] = branch[1]
    plan_ref[2] = arrives
    plan_ref[3] = step
    plan_ref[4] = place
    for i in range(5, 8):
        plan_ref[i] = zero


def project_kernel(
    rows, head_size, join_ref, hidden_ref, gain_ref, weight_ref,
    keep_ref, send_ref, only_ref, way_ref, plan_ref, scaled_ref,
):
    chips = rows // 2

    @pl.when(pl.program_id(0) == 0)
    def _():
        write_plan(rows, join_ref, only_ref, way_ref, plan_ref)
        scaled = hidden_ref[...].astype(jnp.float32) * gain_ref[...].astype(jnp.float32)[None, :]
        scaled = scaled.astype(jnp.bfloat16)
        count = STEPS * rows
        to = lax.broadcasted_iota(jnp.int32, (count, count), 0)
        given = lax.broadcasted_iota(jnp.int32, (count, count), 1)
        core = (to // (STEPS * chips)) ^ (lax.axis_index("rows") & 1)
        wanted = lax.rem(to // chips, STEPS) * rows + lax.rem(to, chips) * 2 + core
        shuffle = jnp.where(given == wanted, 1.0, 0.0).astype(jnp.bfloat16)
        scaled_ref[...] = jnp.dot(
            shuffle, scaled, preferred_element_type=jnp.float32
        ).astype(jnp.bfloat16)

    product = jnp.dot(scaled_ref[...], weight_ref[...], preferred_element_type=jnp.float32)
    for h in range(weight_ref.shape[1] // head_size):
        piece = product[:, h * head_size:(h + 1) * head_size]
        for s in range(STEPS):
            keep_ref[:, s, h, :] = piece[s * chips:(s + 1) * chips]
            start = (STEPS + s) * chips
            send_ref[:, s, h, :] = piece[start:start + chips]


def project(rows, head_size, join_list, hidden, norm_gain, query_weight):
    width, columns = query_weight.shape
    chips = rows // 2
    heads_here = columns // head_size
    parts = 4 if heads_here % 32 == 0 else 1
    smem = pl.BlockSpec(memory_space=pltpu.SMEM)
    block = pl.BlockSpec((chips, STEPS, heads_here // parts, head_size), lambda i: (0, 0, i, 0))
    sums = jax.ShapeDtypeStruct((chips, STEPS, heads_here, head_size), jnp.float32)
    return pl.pallas_call(
        functools.partial(project_kernel, rows, head_size),
        grid=(parts,),
        out_shape=(
            sums,
            sums,
            jax.ShapeDtypeStruct((1,), jnp.int32),
            jax.ShapeDtypeStruct((1,), jnp.int32),
            jax.ShapeDtypeStruct((8,), jnp.int32),
        ),
        in_specs=[
            smem,
            pl.BlockSpec((STEPS * rows, width), lambda i: (0, 0)),
            pl.BlockSpec((width,), lambda i: (0,)),
            pl.BlockSpec((width, columns // parts), lambda i: (0, i)),
        ],
        out_specs=(block, block, smem, smem, smem),
        scratch_shapes=[pltpu.VMEM((STEPS * rows, width), jnp.bfloat16)],
        compiler_params=pltpu.CompilerParams(vmem_limit_bytes=60 * 1024 * 1024),
        cost_estimate=pl.CostEstimate(
            flops=2 * STEPS * rows * width * columns,
            bytes_accessed=2 * width * columns + 4 * STEPS * rows * columns,
            transcendentals=0,
        ),
        name="project",
    )(join_list, hidden.reshape(STEPS * rows, width), norm_gain, query_weight)


def transfer(branch, rows, *tiles):
    branches = [lambda *blocks: jnp.zeros_like(blocks[0])]

    def keep(index):
        return lambda *blocks: blocks[index]

    def send(index, pairs):
        return lambda *blocks: lax.ppermute(blocks[index], "rows", pairs)

    for index in range(len(tiles)):
        branches.append(keep(index))
        for key in range(1, rows):
            for low in (True, False):
                pairs = [(i, i ^ key) for i in range(rows) if (i < (i ^ key)) == low]
                branches.append(send(index, pairs))
    return lax.switch(branch, branches, *tiles)


def move_tiles(only, way, plan, join_list, rows, own, other):
    me = lax.axis_index("rows")

    def once(own, other):
        return transfer(only[0], rows, own, other)

    def twice(own, other):
        first = transfer(plan[0], rows, own)
        second = transfer(plan[1], rows, own)
        late = plan[2] == 2
        return jnp.where(plan[2] == 1, first, jnp.where(late, second, jnp.zeros_like(own)))

    def summed(own, other):
        result = jnp.zeros_like(own)
        for s in range(STEPS):
            for j in range(JOINS):
                given = jnp.where(me == join_list[s, j, 0], own, jnp.zeros_like(own))
                given = lax.psum(given, "rows")
                result = jnp.where(me == join_list[s, j, 1], given, result)
        return result

    return lax.switch(way[0], [once, twice, summed], own, other)


def attend_kernel(
    group, head_size, plan_ref, counts_ref, gain_ref, sums_ref, cache_ref, new_ref,
    out_ref, kept_ref, held, fresh, cache_sem, new_sem, kept_sem,
):
    _, kv_here, slots, _, _ = cache_ref.shape
    join_step, join_slot = plan_ref[3], plan_ref[4]
    one, zero = jnp.int32(1), jnp.int32(0)
    joined = join_step < STEPS

    def shown_at(s, i):
        return (i < counts_ref[s, 0]) & ((join_step > s) | (join_slot != i))

    needed = []
    for i in range(slots):
        any_step = shown_at(0, i)
        for s in range(1, STEPS):
            any_step = any_step | shown_at(s, i)
        needed.append(any_step)

    def fetch(h, i):
        return pltpu.make_async_copy(cache_ref.at[0, h, i], held.at[h, i], cache_sem.at[h, i])

    def fetch_new(h):
        return pltpu.make_async_copy(new_ref.at[h], fresh.at[h], new_sem.at[h])

    def keep(h):
        return pltpu.make_async_copy(fresh.at[h], kept_ref.at[h], kept_sem.at[h])

    for h in range(kv_here):
        for i in range(slots):
            pl.when(needed[i])(fetch(h, i).start)
        pl.when(joined)(fetch_new(h).start)

    @pl.when(jnp.logical_not(joined))
    def _():
        fresh[...] = jnp.zeros_like(fresh)

    step = lax.broadcasted_iota(jnp.int32, (STEPS * group, 1), 0) // group
    raw = sums_ref[0]
    for k in range(1, sums_ref.shape[0]):
        raw = raw + sums_ref[k]
    gain = gain_ref[...].astype(jnp.float32)
    for h in range(kv_here):
        rows = raw[:, h * group:(h + 1) * group].reshape(STEPS * group, head_size)
        queries = (
            rows
            * lax.rsqrt(jnp.mean(rows * rows, axis=-1, keepdims=True) + epsilon)
            * gain
        ).astype(jnp.bfloat16)
        for i in range(slots):
            pl.when(needed[i])(fetch(h, i).wait)
        pl.when(joined)(fetch_new(h).wait)
        keep(h).start()

        def scores_of(keys, shown):
            scores = lax.dot_general(
                queries, keys, (((1,), (1,)), ((), ())), preferred_element_type=jnp.float32
            ) * (1.0 / math.sqrt(head_size))
            usable = jnp.where(step == 1, shown[1], shown[0]) > 0
            return jnp.where(usable, scores, -1e30)

        all_scores = []
        for i in range(slots):
            shown = [jnp.where(shown_at(s, i), one, zero) for s in range(STEPS)]
            all_scores.append(scores_of(held[h, i, :, :head_size], shown))
        shown = [jnp.where(join_step <= s, one, zero) for s in range(STEPS)]
        all_scores.append(scores_of(fresh[h, :, :head_size], shown))
        highest = all_scores[0].max(axis=-1, keepdims=True)
        for scores in all_scores[1:]:
            highest = jnp.maximum(highest, scores.max(axis=-1, keepdims=True))
        exponents = [jnp.exp(scores - highest) for scores in all_scores]
        total = exponents[0].sum(axis=-1, keepdims=True)
        for exponent in exponents[1:]:
            total = total + exponent.sum(axis=-1, keepdims=True)
        context = jnp.zeros((STEPS * group, head_size), jnp.float32)
        for i, exponent in enumerate(exponents):
            probs = (exponent / total).astype(jnp.bfloat16)
            if i < slots:
                values = held[h, i, :, head_size:]
                values = jnp.where(needed[i], values, jnp.zeros_like(values))
            else:
                values = fresh[h, :, head_size:]
            context = context + jnp.dot(probs, values, preferred_element_type=jnp.float32)
        for g in range(group):
            for s in range(STEPS):
                r = s * group + g
                start = (h * group + g) * head_size
                out_ref[s:s + 1, start:start + head_size] = context[r:r + 1]
    for h in range(kv_here):
        keep(h).wait()


def attend(plan, counts, query_gain, sums, kv_cache, arrived):
    _, kv_here, slots, tile_len, width = kv_cache.shape
    _, _, heads_here, head_size = sums.shape
    group = heads_here // kv_here
    smem = pl.BlockSpec(memory_space=pltpu.SMEM)
    vmem = pl.BlockSpec(memory_space=pltpu.VMEM)
    hbm = pl.BlockSpec(memory_space=pl.ANY)
    return pl.pallas_call(
        functools.partial(attend_kernel, group, head_size),
        in_specs=[smem, smem, vmem, vmem, hbm, hbm],
        out_specs=(vmem, hbm),
        out_shape=(
            jax.ShapeDtypeStruct((STEPS, heads_here * head_size), jnp.float32),
            jax.ShapeDtypeStruct(arrived.shape, jnp.bfloat16),
        ),
        scratch_shapes=[
            pltpu.VMEM((kv_here, slots, tile_len, width), jnp.bfloat16),
            pltpu.VMEM((kv_here, tile_len, width), jnp.bfloat16),
            pltpu.SemaphoreType.DMA((kv_here, slots)),
            pltpu.SemaphoreType.DMA((kv_here,)),
            pltpu.SemaphoreType.DMA((kv_here,)),
        ],
        compiler_params=pltpu.CompilerParams(vmem_limit_bytes=53 * 1024 * 1024),
        cost_estimate=pl.CostEstimate(
            flops=4 * kv_here * (slots + 1) * tile_len * width * group,
            bytes_accessed=kv_here * (slots + 2) * tile_len * width * 2,
            transcendentals=kv_here * (slots + 1) * tile_len * group * STEPS,
        ),
        name="attend",
    )(plan, counts, query_gain.reshape(1, head_size), sums, kv_cache, arrived)


def on_device(
    rows,
    heads,
    hidden,
    norm_gain,
    query_weight,
    query_gain,
    out_weight,
    attn_gate,
    kv_cache,
    new_tiles,
    counts,
    join_list,
):
    width = hidden.shape[2]
    me = lax.axis_index("rows")
    odd = (me & 1) > 0
    chips = rows // 2
    own_tile = new_tiles[0]

    def across(block, axis, size, key):
        return lax.ppermute(block, axis, [(i, i ^ key) for i in range(size)])

    same_core = [list(range(core, rows, 2)) for core in range(2)]

    def between_chips(blocks):
        return lax.all_to_all(blocks, "rows", 0, 0, axis_index_groups=same_core, tiled=True)

    other_tile = across(own_tile, "rows", rows, 1)
    head_size = kv_cache.shape[4] // 2
    columns = query_weight.shape[1]
    keep, send, only, way, plan = project(
        rows, head_size, join_list, hidden, norm_gain, query_weight
    )
    sums = between_chips(keep + across(send, "rows", rows, 1))
    arrived = move_tiles(only, way, plan, join_list, rows, own_tile, other_tile)
    context, arrived = attend(plan, counts, query_gain, sums, kv_cache, arrived)
    context = context.astype(jnp.bfloat16)
    mine = between_chips(jnp.broadcast_to(context, (chips, STEPS, columns)))
    theirs = across(mine, "rows", rows, 1)
    gathered = jnp.stack(
        [jnp.where(odd, theirs, mine), jnp.where(odd, mine, theirs)], axis=1
    )
    gathered = gathered.transpose(2, 0, 1, 3).reshape(STEPS * rows, columns)
    projected = jnp.dot(gathered, out_weight, preferred_element_type=jnp.float32)
    key = 1
    while key < heads:
        projected = projected + across(projected, "heads", heads, key)
        key *= 2
    projected = projected.reshape(STEPS, rows, width)
    mixed = (hidden.astype(jnp.float32) + jnp.tanh(attn_gate[0]) * projected).astype(jnp.bfloat16)
    return mixed, arrived[None]


def solution(mesh):
    in_specs = (
        P(None, None, "rows"),
        P("rows"),
        P("rows", "heads"),
        P(),
        P("heads", "rows"),
        P(),
        P("rows", "heads", None, None, None),
        P("rows", "heads", None, None),
        P(None, "rows"),
        P(),
    )
    out_specs = (P(None, None, "rows"), P("rows", "heads", None, None))
    body = functools.partial(on_device, mesh.shape["rows"], mesh.shape["heads"])
    return jax.shard_map(
        body, mesh=mesh, in_specs=in_specs, out_specs=out_specs, check_vma=False
    )
```

```python
import functools
import math

import jax
import jax.numpy as jnp
from jax import lax
from jax.experimental import pallas as pl
from jax.experimental.pallas import tpu as pltpu
from jax.sharding import PartitionSpec as P

STEPS = 2
JOINS = 2
TOTAL = STEPS * JOINS

epsilon = 1e-05

ROUNDS = [(0, 0, 0, 0), (0, 1, 0, 0), (0, 0, 1, 0), (0, 0, 0, 1),
          (0, 1, 1, 0), (0, 1, 0, 1), (0, 0, 1, 1), (0, 1, 1, 1)]


def write_plan(rows, join_ref, only_ref, plan_ref):
    me = lax.axis_index("rows")
    source, target, slot = [], [], []
    for s in range(STEPS):
        for j in range(JOINS):
            source.append(join_ref[s, j, 0])
            target.append(join_ref[s, j, 1])
            slot.append(join_ref[s, j, 2])
    one, zero = jnp.int32(1), jnp.int32(0)

    busy = []
    for i in range(TOTAL):
        for sender in (source[i], source[i] ^ 1):
            hit = zero
            for j in range(TOTAL):
                if j != i:
                    hit = hit | jnp.where(sender == target[j], one, zero)
            busy.append(hit)
    same = {}
    for i in range(TOTAL):
        for j in range(i + 1, TOTAL):
            same[i, j] = jnp.where(source[i] == (source[j] ^ 1), one, zero)
    single = zero
    swap = [zero] * TOTAL
    choices = sorted(range(2 ** TOTAL), key=lambda m: (-bin(m).count("1"), m))
    for m in choices:
        bits = [(m >> i) & 1 for i in range(TOTAL)]
        bad = zero
        for i in range(TOTAL):
            bad = bad | busy[2 * i + bits[i]]
        for (i, j), value in same.items():
            if bits[i] != bits[j]:
                bad = bad | value
        good = bad == 0
        single = jnp.where(good, one, single)
        swap = [jnp.where(good, jnp.int32(b), w) for b, w in zip(bits, swap)]

    clash = {}
    for i in range(TOTAL):
        for j in range(i + 1, TOTAL):
            both = (source[i] == target[j]) | (source[j] == target[i])
            clash[i, j] = jnp.where(both, one, zero)
    best = [zero] * TOTAL
    double = zero
    for rounds in reversed(ROUNDS):
        bad = zero
        for (i, j), value in clash.items():
            if rounds[i] == rounds[j]:
                bad = bad | value
        good = bad == 0
        double = jnp.where(good, one, double)
        best = [jnp.where(good, jnp.int32(r), b) for r, b in zip(rounds, best)]

    def kind_of(s, t):
        key = s ^ t
        return jnp.where(key == 0, 1, 2 * key + jnp.where(s < t, 0, 1))

    only, branch = zero, [zero, zero]
    arrives, step, place = zero, jnp.int32(STEPS), zero
    for i in range(TOTAL):
        s, t = source[i], target[i]
        sender = s ^ swap[i]
        part = (me == sender) | (me == t)
        only = jnp.where(part, kind_of(sender, t) + swap[i] * (2 * rows - 1), only)
        part = (me == s) | (me == t)
        for r in range(2):
            branch[r] = jnp.where(part & (best[i] == r), kind_of(s, t), branch[r])
        here = me == t
        arrives = jnp.where(here, best[i] + 1, arrives)
        step = jnp.where(here, i // JOINS, step)
        place = jnp.where(here, slot[i], place)
    rest = 1 + 2 * (2 * rows - 1)
    rest = jnp.where(double > 0, jnp.int32(rest), jnp.int32(rest + 1))
    only_ref[0] = jnp.where(single > 0, only, rest)
    plan_ref[0] = branch[0]
    plan_ref[1] = branch[1]
    plan_ref[2] = arrives
    plan_ref[3] = step
    plan_ref[4] = place
    for i in range(5, 8):
        plan_ref[i] = zero


def project_kernel(
    rows, head_size, parts, join_ref, hidden_ref, gain_ref, weight_ref,
    keep_ref, send_ref, only_ref, plan_ref, held, hidden, gain, sem, small_sem,
):
    chips = rows // 2
    wide = weight_ref.shape[1] // parts
    fetches = [
        pltpu.make_async_copy(
            weight_ref.at[:, pl.ds(i * wide, wide)], held.at[i], sem.at[i]
        )
        for i in range(parts)
    ]
    small = [
        pltpu.make_async_copy(hidden_ref, hidden, small_sem.at[0]),
        pltpu.make_async_copy(gain_ref, gain, small_sem.at[1]),
    ]
    for fetch in small + fetches:
        fetch.start()
    write_plan(rows, join_ref, only_ref, plan_ref)
    for fetch in small:
        fetch.wait()
    scaled = hidden[...].astype(jnp.float32) * gain[...].astype(jnp.float32)[None, :]
    scaled = scaled.astype(jnp.bfloat16)
    count = STEPS * rows
    to = lax.broadcasted_iota(jnp.int32, (count, count), 0)
    given = lax.broadcasted_iota(jnp.int32, (count, count), 1)
    core = (to // (STEPS * chips)) ^ (lax.axis_index("rows") & 1)
    wanted = lax.rem(to // chips, STEPS) * rows + lax.rem(to, chips) * 2 + core
    shuffle = jnp.where(given == wanted, 1.0, 0.0).astype(jnp.bfloat16)
    scaled = jnp.dot(shuffle, scaled, preferred_element_type=jnp.float32).astype(jnp.bfloat16)
    for i in range(parts):
        fetches[i].wait()
        product = jnp.dot(scaled, held[i], preferred_element_type=jnp.float32)
        for j in range(wide // head_size):
            h = i * (wide // head_size) + j
            piece = product[:, j * head_size:(j + 1) * head_size]
            for s in range(STEPS):
                keep_ref[:, s, h, :] = piece[s * chips:(s + 1) * chips]
                start = (STEPS + s) * chips
                send_ref[:, s, h, :] = piece[start:start + chips]


def project(rows, head_size, join_list, hidden, norm_gain, query_weight):
    width, columns = query_weight.shape
    chips = rows // 2
    heads_here = columns // head_size
    parts = min(2, heads_here)
    smem = pl.BlockSpec(memory_space=pltpu.SMEM)
    vmem = pl.BlockSpec(memory_space=pltpu.VMEM)
    hbm = pl.BlockSpec(memory_space=pltpu.HBM)
    pinned = [
        pltpu.with_memory_space_constraint(x, pltpu.HBM)
        for x in (hidden.reshape(STEPS * rows, width), norm_gain, query_weight)
    ]
    sums = jax.ShapeDtypeStruct((chips, STEPS, heads_here, head_size), jnp.float32)
    return pl.pallas_call(
        functools.partial(project_kernel, rows, head_size, parts),
        out_shape=(
            sums,
            sums,
            jax.ShapeDtypeStruct((1,), jnp.int32),
            jax.ShapeDtypeStruct((8,), jnp.int32),
        ),
        in_specs=[smem, hbm, hbm, hbm],
        out_specs=(vmem, vmem, smem, smem),
        scratch_shapes=[
            pltpu.VMEM((parts, width, columns // parts), jnp.bfloat16),
            pltpu.VMEM((STEPS * rows, width), jnp.bfloat16),
            pltpu.VMEM((width,), jnp.bfloat16),
            pltpu.SemaphoreType.DMA((parts,)),
            pltpu.SemaphoreType.DMA((2,)),
        ],
        compiler_params=pltpu.CompilerParams(vmem_limit_bytes=24 * 1024 * 1024),
        cost_estimate=pl.CostEstimate(
            flops=2 * STEPS * rows * width * columns,
            bytes_accessed=2 * width * columns + 4 * STEPS * rows * columns,
            transcendentals=0,
        ),
        name="project",
    )(join_list, *pinned)


def output_kernel(parts, context_ref, weight_ref, out_ref, held, sem):
    deep = weight_ref.shape[0] // parts
    fetches = [
        pltpu.make_async_copy(weight_ref.at[pl.ds(i * deep, deep)], held.at[i], sem.at[i])
        for i in range(parts)
    ]
    for fetch in fetches:
        fetch.start()
    total = jnp.zeros(out_ref.shape, jnp.float32)
    for i in range(parts):
        fetches[i].wait()
        total = total + jnp.dot(
            context_ref[:, i * deep:(i + 1) * deep],
            held[i],
            preferred_element_type=jnp.float32,
        )
    out_ref[...] = total


def output(context, out_weight):
    deep, width = out_weight.shape
    parts = 8
    vmem = pl.BlockSpec(memory_space=pltpu.VMEM)
    return pl.pallas_call(
        functools.partial(output_kernel, parts),
        out_shape=jax.ShapeDtypeStruct((context.shape[0], width), jnp.float32),
        in_specs=[vmem, pl.BlockSpec(memory_space=pltpu.HBM)],
        out_specs=vmem,
        scratch_shapes=[
            pltpu.VMEM((parts, deep // parts, width), jnp.bfloat16),
            pltpu.SemaphoreType.DMA((parts,)),
        ],
        compiler_params=pltpu.CompilerParams(vmem_limit_bytes=24 * 1024 * 1024),
        cost_estimate=pl.CostEstimate(
            flops=2 * context.size * width,
            bytes_accessed=2 * deep * width + 2 * context.size,
            transcendentals=0,
        ),
        name="output",
    )(context, pltpu.with_memory_space_constraint(out_weight, pltpu.HBM))


def transfer(branch, rows, tiles, others=()):
    branches = [lambda *blocks: jnp.zeros_like(blocks[0])]

    def keep(index):
        return lambda *blocks: blocks[index]

    def send(index, pairs):
        return lambda *blocks: lax.ppermute(blocks[index], "rows", pairs)

    for index in range(len(tiles)):
        branches.append(keep(index))
        for key in range(1, rows):
            for low in (True, False):
                pairs = [(i, i ^ key) for i in range(rows) if (i < (i ^ key)) == low]
                branches.append(send(index, pairs))
    return lax.switch(branch, branches + list(others), *tiles)


def move_tiles(only, plan, join_list, rows, own, other):
    me = lax.axis_index("rows")

    def twice(own, other):
        first = transfer(plan[0], rows, (own,))
        second = transfer(plan[1], rows, (own,))
        late = plan[2] == 2
        return jnp.where(plan[2] == 1, first, jnp.where(late, second, jnp.zeros_like(own)))

    def summed(own, other):
        result = jnp.zeros_like(own)
        for s in range(STEPS):
            for j in range(JOINS):
                given = jnp.where(me == join_list[s, j, 0], own, jnp.zeros_like(own))
                given = lax.psum(given, "rows")
                result = jnp.where(me == join_list[s, j, 1], given, result)
        return result

    return transfer(only[0], rows, (own, other), (twice, summed))


def attend_kernel(
    group, head_size, plan_ref, counts_ref, gain_ref, sums_ref, cache_ref, new_ref,
    out_ref, kept_ref, held, fresh, cache_sem, new_sem, kept_sem,
):
    _, kv_here, slots, _, _ = cache_ref.shape
    join_step, join_slot = plan_ref[3], plan_ref[4]
    one, zero = jnp.int32(1), jnp.int32(0)
    joined = join_step < STEPS

    def shown_at(s, i):
        return (i < counts_ref[s, 0]) & ((join_step > s) | (join_slot != i))

    needed = []
    for i in range(slots):
        any_step = shown_at(0, i)
        for s in range(1, STEPS):
            any_step = any_step | shown_at(s, i)
        needed.append(any_step)

    def fetch(h, i):
        return pltpu.make_async_copy(cache_ref.at[0, h, i], held.at[h, i], cache_sem.at[h, i])

    def fetch_new(h):
        return pltpu.make_async_copy(new_ref.at[h], fresh.at[h], new_sem.at[h])

    def keep(h):
        return pltpu.make_async_copy(fresh.at[h], kept_ref.at[h], kept_sem.at[h])

    for h in range(kv_here):
        for i in range(slots):
            pl.when(needed[i])(fetch(h, i).start)
        pl.when(joined)(fetch_new(h).start)

    @pl.when(jnp.logical_not(joined))
    def _():
        fresh[...] = jnp.zeros_like(fresh)

    step = lax.broadcasted_iota(jnp.int32, (STEPS * group, 1), 0) // group
    raw = sums_ref[0]
    for k in range(1, sums_ref.shape[0]):
        raw = raw + sums_ref[k]
    gain = gain_ref[...].astype(jnp.float32)
    for h in range(kv_here):
        rows = raw[:, h * group:(h + 1) * group].reshape(STEPS * group, head_size)
        queries = (
            rows
            * lax.rsqrt(jnp.mean(rows * rows, axis=-1, keepdims=True) + epsilon)
            * gain
        ).astype(jnp.bfloat16)
        for i in range(slots):
            pl.when(needed[i])(fetch(h, i).wait)
        pl.when(joined)(fetch_new(h).wait)
        keep(h).start()

        def scores_of(keys, shown):
            scores = lax.dot_general(
                queries, keys, (((1,), (1,)), ((), ())), preferred_element_type=jnp.float32
            ) * (1.0 / math.sqrt(head_size))
            usable = jnp.where(step == 1, shown[1], shown[0]) > 0
            return jnp.where(usable, scores, -1e30)

        all_scores = []
        for i in range(slots):
            shown = [jnp.where(shown_at(s, i), one, zero) for s in range(STEPS)]
            all_scores.append(scores_of(held[h, i, :, :head_size], shown))
        shown = [jnp.where(join_step <= s, one, zero) for s in range(STEPS)]
        all_scores.append(scores_of(fresh[h, :, :head_size], shown))
        highest = all_scores[0].max(axis=-1, keepdims=True)
        for scores in all_scores[1:]:
            highest = jnp.maximum(highest, scores.max(axis=-1, keepdims=True))
        exponents = [jnp.exp(scores - highest) for scores in all_scores]
        total = exponents[0].sum(axis=-1, keepdims=True)
        for exponent in exponents[1:]:
            total = total + exponent.sum(axis=-1, keepdims=True)
        context = jnp.zeros((STEPS * group, head_size), jnp.float32)
        for i, exponent in enumerate(exponents):
            probs = (exponent / total).astype(jnp.bfloat16)
            if i < slots:
                values = held[h, i, :, head_size:]
                values = jnp.where(needed[i], values, jnp.zeros_like(values))
            else:
                values = fresh[h, :, head_size:]
            context = context + jnp.dot(probs, values, preferred_element_type=jnp.float32)
        for g in range(group):
            for s in range(STEPS):
                r = s * group + g
                start = (h * group + g) * head_size
                out_ref[s:s + 1, start:start + head_size] = context[r:r + 1]
    for h in range(kv_here):
        keep(h).wait()


def attend(plan, counts, query_gain, sums, kv_cache, arrived):
    _, kv_here, slots, tile_len, width = kv_cache.shape
    _, _, heads_here, head_size = sums.shape
    group = heads_here // kv_here
    smem = pl.BlockSpec(memory_space=pltpu.SMEM)
    vmem = pl.BlockSpec(memory_space=pltpu.VMEM)
    hbm = pl.BlockSpec(memory_space=pltpu.HBM)
    pinned = [pltpu.with_memory_space_constraint(x, pltpu.HBM) for x in (kv_cache, arrived)]
    return pl.pallas_call(
        functools.partial(attend_kernel, group, head_size),
        in_specs=[smem, smem, vmem, vmem, hbm, hbm],
        out_specs=(vmem, hbm),
        out_shape=(
            jax.ShapeDtypeStruct((STEPS, heads_here * head_size), jnp.float32),
            jax.ShapeDtypeStruct(arrived.shape, jnp.bfloat16),
        ),
        scratch_shapes=[
            pltpu.VMEM((kv_here, slots, tile_len, width), jnp.bfloat16),
            pltpu.VMEM((kv_here, tile_len, width), jnp.bfloat16),
            pltpu.SemaphoreType.DMA((kv_here, slots)),
            pltpu.SemaphoreType.DMA((kv_here,)),
            pltpu.SemaphoreType.DMA((kv_here,)),
        ],
        compiler_params=pltpu.CompilerParams(vmem_limit_bytes=40 * 1024 * 1024),
        cost_estimate=pl.CostEstimate(
            flops=4 * kv_here * (slots + 1) * tile_len * width * group,
            bytes_accessed=kv_here * (slots + 2) * tile_len * width * 2,
            transcendentals=kv_here * (slots + 1) * tile_len * group * STEPS,
        ),
        name="attend",
    )(plan, counts, query_gain.reshape(1, head_size), sums, *pinned)


def on_device(
    rows,
    heads,
    hidden,
    norm_gain,
    query_weight,
    query_gain,
    out_weight,
    attn_gate,
    kv_cache,
    new_tiles,
    counts,
    join_list,
):
    width = hidden.shape[2]
    me = lax.axis_index("rows")
    odd = (me & 1) > 0
    chips = rows // 2
    own_tile = new_tiles[0]

    def across(block, axis, size, key):
        return lax.ppermute(block, axis, [(i, i ^ key) for i in range(size)])

    same_core = [list(range(core, rows, 2)) for core in range(2)]

    def between_chips(blocks):
        return lax.all_to_all(blocks, "rows", 0, 0, axis_index_groups=same_core, tiled=True)

    other_tile = across(own_tile, "rows", rows, 1)
    head_size = kv_cache.shape[4] // 2
    columns = query_weight.shape[1]
    keep, send, only, plan = project(
        rows, head_size, join_list, hidden, norm_gain, query_weight
    )
    sums = between_chips(keep + across(send, "rows", rows, 1))
    arrived = move_tiles(only, plan, join_list, rows, own_tile, other_tile)
    context, arrived = attend(plan, counts, query_gain, sums, kv_cache, arrived)
    context = context.astype(jnp.bfloat16)
    mine = between_chips(jnp.broadcast_to(context, (chips, STEPS, columns)))
    theirs = across(mine, "rows", rows, 1)
    gathered = jnp.stack(
        [jnp.where(odd, theirs, mine), jnp.where(odd, mine, theirs)], axis=1
    )
    gathered = gathered.transpose(2, 0, 1, 3).reshape(STEPS * rows, columns)
    projected = output(gathered, out_weight)
    key = 1
    while key < heads:
        projected = projected + across(projected, "heads", heads, key)
        key *= 2
    projected = projected.reshape(STEPS, rows, width)
    mixed = (hidden.astype(jnp.float32) + jnp.tanh(attn_gate[0]) * projected).astype(jnp.bfloat16)
    return mixed, arrived[None]


def solution(mesh):
    in_specs = (
        P(None, None, "rows"),
        P("rows"),
        P("rows", "heads"),
        P(),
        P("heads", "rows"),
        P(),
        P("rows", "heads", None, None, None),
        P("rows", "heads", None, None),
        P(None, "rows"),
        P(),
    )
    out_specs = (P(None, None, "rows"), P("rows", "heads", None, None))
    body = functools.partial(on_device, mesh.shape["rows"], mesh.shape["heads"])
    return jax.shard_map(
        body, mesh=mesh, in_specs=in_specs, out_specs=out_specs, check_vma=False
    )
```

```python
import functools
import math

import jax
import jax.numpy as jnp
from jax import lax
from jax.experimental import pallas as pl
from jax.experimental.pallas import tpu as pltpu
from jax.sharding import PartitionSpec as P

STEPS = 2
JOINS = 2
TOTAL = STEPS * JOINS

epsilon = 1e-05

ROUNDS = [(0, 0, 0, 0), (0, 1, 0, 0), (0, 0, 1, 0), (0, 0, 0, 1),
          (0, 1, 1, 0), (0, 1, 0, 1), (0, 0, 1, 1), (0, 1, 1, 1)]


def write_plan(rows, join_ref, only_ref, plan_ref):
    me = lax.axis_index("rows")
    source, target, slot = [], [], []
    for s in range(STEPS):
        for j in range(JOINS):
            source.append(join_ref[s, j, 0])
            target.append(join_ref[s, j, 1])
            slot.append(join_ref[s, j, 2])
    one, zero = jnp.int32(1), jnp.int32(0)

    busy = []
    for i in range(TOTAL):
        for sender in (source[i], source[i] ^ 1):
            hit = zero
            for j in range(TOTAL):
                if j != i:
                    hit = hit | jnp.where(sender == target[j], one, zero)
            busy.append(hit)
    same = {}
    for i in range(TOTAL):
        for j in range(i + 1, TOTAL):
            same[i, j] = jnp.where(source[i] == (source[j] ^ 1), one, zero)
    single = zero
    swap = [zero] * TOTAL
    choices = sorted(range(2 ** TOTAL), key=lambda m: (-bin(m).count("1"), m))
    for m in choices:
        bits = [(m >> i) & 1 for i in range(TOTAL)]
        bad = zero
        for i in range(TOTAL):
            bad = bad | busy[2 * i + bits[i]]
        for (i, j), value in same.items():
            if bits[i] != bits[j]:
                bad = bad | value
        good = bad == 0
        single = jnp.where(good, one, single)
        swap = [jnp.where(good, jnp.int32(b), w) for b, w in zip(bits, swap)]

    clash = {}
    for i in range(TOTAL):
        for j in range(i + 1, TOTAL):
            both = (source[i] == target[j]) | (source[j] == target[i])
            clash[i, j] = jnp.where(both, one, zero)
    best = [zero] * TOTAL
    double = zero
    for rounds in reversed(ROUNDS):
        bad = zero
        for (i, j), value in clash.items():
            if rounds[i] == rounds[j]:
                bad = bad | value
        good = bad == 0
        double = jnp.where(good, one, double)
        best = [jnp.where(good, jnp.int32(r), b) for r, b in zip(rounds, best)]

    def kind_of(s, t):
        key = s ^ t
        return jnp.where(key == 0, 1, 2 * key + jnp.where(s < t, 0, 1))

    only, branch = zero, [zero, zero]
    arrives, step, place = zero, jnp.int32(STEPS), zero
    for i in range(TOTAL):
        s, t = source[i], target[i]
        sender = s ^ swap[i]
        part = (me == sender) | (me == t)
        only = jnp.where(part, kind_of(sender, t) + swap[i] * (2 * rows - 1), only)
        part = (me == s) | (me == t)
        for r in range(2):
            branch[r] = jnp.where(part & (best[i] == r), kind_of(s, t), branch[r])
        here = me == t
        arrives = jnp.where(here, best[i] + 1, arrives)
        step = jnp.where(here, i // JOINS, step)
        place = jnp.where(here, slot[i], place)
    rest = 1 + 2 * (2 * rows - 1)
    rest = jnp.where(double > 0, jnp.int32(rest), jnp.int32(rest + 1))
    only_ref[0] = jnp.where(single > 0, only, rest)
    plan_ref[0] = branch[0]
    plan_ref[1] = branch[1]
    plan_ref[2] = arrives
    plan_ref[3] = step
    plan_ref[4] = place
    for i in range(5, 8):
        plan_ref[i] = zero


def project_kernel(
    rows, head_size, parts, join_ref, hidden_ref, gain_ref, weight_ref,
    keep_ref, send_ref, only_ref, plan_ref, held, hidden, gain, sem, small_sem,
):
    chips = rows // 2
    wide = weight_ref.shape[1] // parts
    fetches = [
        pltpu.make_async_copy(
            weight_ref.at[:, pl.ds(i * wide, wide)], held.at[i], sem.at[i]
        )
        for i in range(parts)
    ]
    small = [
        pltpu.make_async_copy(hidden_ref, hidden, small_sem.at[0]),
        pltpu.make_async_copy(gain_ref, gain, small_sem.at[1]),
    ]
    for fetch in small + fetches:
        fetch.start()
    write_plan(rows, join_ref, only_ref, plan_ref)
    for fetch in small:
        fetch.wait()
    scaled = hidden[...].astype(jnp.float32) * gain[...].astype(jnp.float32)[None, :]
    scaled = scaled.astype(jnp.bfloat16)
    count = STEPS * rows
    to = lax.broadcasted_iota(jnp.int32, (count, count), 0)
    given = lax.broadcasted_iota(jnp.int32, (count, count), 1)
    core = (to // (STEPS * chips)) ^ (lax.axis_index("rows") & 1)
    wanted = lax.rem(to // chips, STEPS) * rows + lax.rem(to, chips) * 2 + core
    shuffle = jnp.where(given == wanted, 1.0, 0.0).astype(jnp.bfloat16)
    scaled = jnp.dot(shuffle, scaled, preferred_element_type=jnp.float32).astype(jnp.bfloat16)
    for i in range(parts):
        fetches[i].wait()
        product = jnp.dot(scaled, held[i], preferred_element_type=jnp.float32)
        for j in range(wide // head_size):
            h = i * (wide // head_size) + j
            piece = product[:, j * head_size:(j + 1) * head_size]
            for s in range(STEPS):
                keep_ref[:, s, h, :] = piece[s * chips:(s + 1) * chips]
                start = (STEPS + s) * chips
                send_ref[:, s, h, :] = piece[start:start + chips]


def project(rows, head_size, join_list, hidden, norm_gain, query_weight):
    width, columns = query_weight.shape
    chips = rows // 2
    heads_here = columns // head_size
    parts = min(2, heads_here)
    smem = pl.BlockSpec(memory_space=pltpu.SMEM)
    vmem = pl.BlockSpec(memory_space=pltpu.VMEM)
    hbm = pl.BlockSpec(memory_space=pltpu.HBM)
    pinned = [
        pltpu.with_memory_space_constraint(x, pltpu.HBM)
        for x in (hidden.reshape(STEPS * rows, width), norm_gain, query_weight)
    ]
    sums = jax.ShapeDtypeStruct((chips, STEPS, heads_here, head_size), jnp.float32)
    return pl.pallas_call(
        functools.partial(project_kernel, rows, head_size, parts),
        out_shape=(
            sums,
            sums,
            jax.ShapeDtypeStruct((1,), jnp.int32),
            jax.ShapeDtypeStruct((8,), jnp.int32),
        ),
        in_specs=[smem, hbm, hbm, hbm],
        out_specs=(vmem, vmem, smem, smem),
        scratch_shapes=[
            pltpu.VMEM((parts, width, columns // parts), jnp.bfloat16),
            pltpu.VMEM((STEPS * rows, width), jnp.bfloat16),
            pltpu.VMEM((width,), jnp.bfloat16),
            pltpu.SemaphoreType.DMA((parts,)),
            pltpu.SemaphoreType.DMA((2,)),
        ],
        compiler_params=pltpu.CompilerParams(vmem_limit_bytes=24 * 1024 * 1024),
        cost_estimate=pl.CostEstimate(
            flops=2 * STEPS * rows * width * columns,
            bytes_accessed=2 * width * columns + 4 * STEPS * rows * columns,
            transcendentals=0,
        ),
        name="project",
    )(join_list, *pinned)


def output_kernel(parts, context_ref, weight_ref, out_ref, held, sem):
    deep = weight_ref.shape[0] // parts
    fetches = [
        pltpu.make_async_copy(weight_ref.at[pl.ds(i * deep, deep)], held.at[i], sem.at[i])
        for i in range(parts)
    ]
    for fetch in fetches:
        fetch.start()
    total = jnp.zeros(out_ref.shape, jnp.float32)
    for i in range(parts):
        fetches[i].wait()
        total = total + jnp.dot(
            context_ref[:, i * deep:(i + 1) * deep],
            held[i],
            preferred_element_type=jnp.float32,
        )
    out_ref[...] = total


def output(context, out_weight):
    deep, width = out_weight.shape
    parts = 8
    vmem = pl.BlockSpec(memory_space=pltpu.VMEM)
    return pl.pallas_call(
        functools.partial(output_kernel, parts),
        out_shape=jax.ShapeDtypeStruct((context.shape[0], width), jnp.float32),
        in_specs=[vmem, pl.BlockSpec(memory_space=pltpu.HBM)],
        out_specs=vmem,
        scratch_shapes=[
            pltpu.VMEM((parts, deep // parts, width), jnp.bfloat16),
            pltpu.SemaphoreType.DMA((parts,)),
        ],
        compiler_params=pltpu.CompilerParams(vmem_limit_bytes=24 * 1024 * 1024),
        cost_estimate=pl.CostEstimate(
            flops=2 * context.size * width,
            bytes_accessed=2 * deep * width + 2 * context.size,
            transcendentals=0,
        ),
        name="output",
    )(context, pltpu.with_memory_space_constraint(out_weight, pltpu.HBM))


def transfer(branch, rows, tiles, others=()):
    branches = [lambda *blocks: jnp.zeros_like(blocks[0])]

    def keep(index):
        return lambda *blocks: blocks[index]

    def send(index, pairs):
        return lambda *blocks: lax.ppermute(blocks[index], "rows", pairs)

    for index in range(len(tiles)):
        branches.append(keep(index))
        for key in range(1, rows):
            for low in (True, False):
                pairs = [(i, i ^ key) for i in range(rows) if (i < (i ^ key)) == low]
                branches.append(send(index, pairs))
    return lax.switch(branch, branches + list(others), *tiles)


def move_tiles(only, plan, join_list, rows, own, other):
    me = lax.axis_index("rows")

    def twice(own, other):
        first = transfer(plan[0], rows, (own,))
        second = transfer(plan[1], rows, (own,))
        late = plan[2] == 2
        return jnp.where(plan[2] == 1, first, jnp.where(late, second, jnp.zeros_like(own)))

    def summed(own, other):
        result = jnp.zeros_like(own)
        for s in range(STEPS):
            for j in range(JOINS):
                given = jnp.where(me == join_list[s, j, 0], own, jnp.zeros_like(own))
                given = lax.psum(given, "rows")
                result = jnp.where(me == join_list[s, j, 1], given, result)
        return result

    return transfer(only[0], rows, (own, other), (twice, summed))


def attend_kernel(
    group, head_size, plan_ref, counts_ref, gain_ref, sums_ref, cache_ref, new_ref,
    out_ref, kept_ref, held, fresh, more, part, cache_sem, new_sem, kept_sem,
):
    _, kv_here, slots, _, _ = cache_ref.shape
    join_step, join_slot = plan_ref[3], plan_ref[4]
    one, zero = jnp.int32(1), jnp.int32(0)
    joined = join_step < STEPS

    def shown_at(s, i):
        return (i < counts_ref[s, 0]) & ((join_step > s) | (join_slot != i))

    needed = []
    for i in range(slots):
        any_step = shown_at(0, i)
        for s in range(1, STEPS):
            any_step = any_step | shown_at(s, i)
        needed.append(any_step)

    needed_there = zero
    for i in range(slots):
        needed_there = needed_there | jnp.where(needed[i] & (join_slot == i), one, zero)
    landed = joined & (needed_there == 0)
    extra = joined & (needed_there > 0)

    def fetch(h, i):
        return pltpu.make_async_copy(cache_ref.at[0, h, i], held.at[h, i], cache_sem.at[h, i])

    def fetch_new(h):
        return pltpu.make_async_copy(new_ref.at[h], fresh.at[h], new_sem.at[h])

    def fetch_in_place(h):
        return pltpu.make_async_copy(new_ref.at[h], held.at[h, join_slot], new_sem.at[h])

    def keep(h):
        return pltpu.make_async_copy(fresh.at[h], kept_ref.at[h], kept_sem.at[h])

    def keep_in_place(h):
        return pltpu.make_async_copy(held.at[h, join_slot], kept_ref.at[h], kept_sem.at[h])

    for h in range(kv_here):
        for i in range(slots):
            pl.when(needed[i])(fetch(h, i).start)
        pl.when(extra)(fetch_new(h).start)
        pl.when(landed)(fetch_in_place(h).start)

    @pl.when(jnp.logical_not(joined))
    def _():
        fresh[...] = jnp.zeros_like(fresh)

    step = lax.broadcasted_iota(jnp.int32, (STEPS * group, 1), 0) // group
    raw = sums_ref[0]
    for k in range(1, sums_ref.shape[0]):
        raw = raw + sums_ref[k]
    gain = gain_ref[...].astype(jnp.float32)
    for h in range(kv_here):
        rows = raw[:, h * group:(h + 1) * group].reshape(STEPS * group, head_size)
        queries = (
            rows
            * lax.rsqrt(jnp.mean(rows * rows, axis=-1, keepdims=True) + epsilon)
            * gain
        ).astype(jnp.bfloat16)
        for i in range(slots):
            pl.when(needed[i])(fetch(h, i).wait)
        pl.when(extra)(fetch_new(h).wait)
        pl.when(landed)(fetch_in_place(h).wait)
        pl.when(landed)(keep_in_place(h).start)
        pl.when(jnp.logical_not(landed))(keep(h).start)

        def scores_of(keys, shown):
            scores = lax.dot_general(
                queries, keys, (((1,), (1,)), ((), ())), preferred_element_type=jnp.float32
            ) * (1.0 / math.sqrt(head_size))
            usable = jnp.where(step == 1, shown[1], shown[0]) > 0
            return jnp.where(usable, scores, -1e30)

        all_scores = []
        for i in range(slots):
            shown = [
                jnp.where(
                    shown_at(s, i) | (landed & (join_slot == i) & (join_step <= s)), one, zero
                )
                for s in range(STEPS)
            ]
            all_scores.append(scores_of(held[h, i, :, :head_size], shown))
        shown = [jnp.where(join_step <= s, one, zero) for s in range(STEPS)]

        @pl.when(extra)
        def _():
            more[...] = scores_of(fresh[h, :, :head_size], shown)

        @pl.when(jnp.logical_not(extra))
        def _():
            more[...] = jnp.full_like(more, -1e30)

        all_scores.append(more[...])
        highest = all_scores[0].max(axis=-1, keepdims=True)
        for scores in all_scores[1:]:
            highest = jnp.maximum(highest, scores.max(axis=-1, keepdims=True))
        exponents = [jnp.exp(scores - highest) for scores in all_scores]
        total = exponents[0].sum(axis=-1, keepdims=True)
        for exponent in exponents[1:]:
            total = total + exponent.sum(axis=-1, keepdims=True)
        context = jnp.zeros((STEPS * group, head_size), jnp.float32)
        for i in range(slots):
            probs = (exponents[i] / total).astype(jnp.bfloat16)
            values = held[h, i, :, head_size:]
            filled = needed[i] | (landed & (join_slot == i))
            values = jnp.where(filled, values, jnp.zeros_like(values))
            context = context + jnp.dot(probs, values, preferred_element_type=jnp.float32)
        part[...] = context

        @pl.when(extra)
        def _():
            probs = (exponents[slots] / total).astype(jnp.bfloat16)
            part[...] += jnp.dot(
                probs, fresh[h, :, head_size:], preferred_element_type=jnp.float32
            )

        context = part[...]
        for g in range(group):
            for s in range(STEPS):
                r = s * group + g
                start = (h * group + g) * head_size
                out_ref[s:s + 1, start:start + head_size] = context[r:r + 1]
    for h in range(kv_here):
        keep(h).wait()


def attend(plan, counts, query_gain, sums, kv_cache, arrived):
    _, kv_here, slots, tile_len, width = kv_cache.shape
    _, _, heads_here, head_size = sums.shape
    group = heads_here // kv_here
    smem = pl.BlockSpec(memory_space=pltpu.SMEM)
    vmem = pl.BlockSpec(memory_space=pltpu.VMEM)
    hbm = pl.BlockSpec(memory_space=pltpu.HBM)
    pinned = [pltpu.with_memory_space_constraint(x, pltpu.HBM) for x in (kv_cache, arrived)]
    return pl.pallas_call(
        functools.partial(attend_kernel, group, head_size),
        in_specs=[smem, smem, vmem, vmem, hbm, hbm],
        out_specs=(vmem, hbm),
        out_shape=(
            jax.ShapeDtypeStruct((STEPS, heads_here * head_size), jnp.float32),
            jax.ShapeDtypeStruct(arrived.shape, jnp.bfloat16),
        ),
        scratch_shapes=[
            pltpu.VMEM((kv_here, slots, tile_len, width), jnp.bfloat16),
            pltpu.VMEM((kv_here, tile_len, width), jnp.bfloat16),
            pltpu.VMEM((STEPS * group, tile_len), jnp.float32),
            pltpu.VMEM((STEPS * group, head_size), jnp.float32),
            pltpu.SemaphoreType.DMA((kv_here, slots)),
            pltpu.SemaphoreType.DMA((kv_here,)),
            pltpu.SemaphoreType.DMA((kv_here,)),
        ],
        compiler_params=pltpu.CompilerParams(vmem_limit_bytes=40 * 1024 * 1024),
        cost_estimate=pl.CostEstimate(
            flops=4 * kv_here * (slots + 1) * tile_len * width * group,
            bytes_accessed=kv_here * (slots + 2) * tile_len * width * 2,
            transcendentals=kv_here * (slots + 1) * tile_len * group * STEPS,
        ),
        name="attend",
    )(plan, counts, query_gain.reshape(1, head_size), sums, *pinned)


def on_device(
    rows,
    heads,
    hidden,
    norm_gain,
    query_weight,
    query_gain,
    out_weight,
    attn_gate,
    kv_cache,
    new_tiles,
    counts,
    join_list,
):
    width = hidden.shape[2]
    me = lax.axis_index("rows")
    odd = (me & 1) > 0
    chips = rows // 2
    own_tile = new_tiles[0]

    def across(block, axis, size, key):
        return lax.ppermute(block, axis, [(i, i ^ key) for i in range(size)])

    same_core = [list(range(core, rows, 2)) for core in range(2)]

    def between_chips(blocks):
        return lax.all_to_all(blocks, "rows", 0, 0, axis_index_groups=same_core, tiled=True)

    other_tile = across(own_tile, "rows", rows, 1)
    head_size = kv_cache.shape[4] // 2
    columns = query_weight.shape[1]
    keep, send, only, plan = project(
        rows, head_size, join_list, hidden, norm_gain, query_weight
    )
    sums = between_chips(keep + across(send, "rows", rows, 1))
    arrived = move_tiles(only, plan, join_list, rows, own_tile, other_tile)
    context, arrived = attend(plan, counts, query_gain, sums, kv_cache, arrived)
    context = context.astype(jnp.bfloat16)
    mine = between_chips(jnp.broadcast_to(context, (chips, STEPS, columns)))
    theirs = across(mine, "rows", rows, 1)
    gathered = jnp.stack(
        [jnp.where(odd, theirs, mine), jnp.where(odd, mine, theirs)], axis=1
    )
    gathered = gathered.transpose(2, 0, 1, 3).reshape(STEPS * rows, columns)
    projected = output(gathered, out_weight)
    key = 1
    while key < heads:
        projected = projected + across(projected, "heads", heads, key)
        key *= 2
    projected = projected.reshape(STEPS, rows, width)
    mixed = (hidden.astype(jnp.float32) + jnp.tanh(attn_gate[0]) * projected).astype(jnp.bfloat16)
    return mixed, arrived[None]


def solution(mesh):
    in_specs = (
        P(None, None, "rows"),
        P("rows"),
        P("rows", "heads"),
        P(),
        P("heads", "rows"),
        P(),
        P("rows", "heads", None, None, None),
        P("rows", "heads", None, None),
        P(None, "rows"),
        P(),
    )
    out_specs = (P(None, None, "rows"), P("rows", "heads", None, None))
    body = functools.partial(on_device, mesh.shape["rows"], mesh.shape["heads"])
    return jax.shard_map(
        body, mesh=mesh, in_specs=in_specs, out_specs=out_specs, check_vma=False
    )
```
